128 devices in a mesh: dp: 8 (over y, x_lo), row: 16 (over z, x_hi, core).
Axes of the slice: x: 4 (x_hi: 2, x_lo: 2; x = x_hi * 2 + x_lo), y: 4, z: 4, core: 2. Of those that a mesh axis runs over, the one named last changes fastest.
Arguments:
- fields: bfloat16 [8, 128, 360, 768], P('dp', 'row'), may hold values from -6 to 6
- cotangent: bfloat16 [8, 128, 360, 768], P('dp', 'row'), may hold values from -6 to 6
- norm_gain: float32 [768], replicated, may hold values from 0.5 to 1.5
- weights: bfloat16 [2, 2, 8, 96, 96], replicated, may hold values from -0.4375 to 0.4375
- biases: float32 [2, 2, 768], replicated, may hold values from -3 to 3
- cutoffs: int32 [16], replicated, may hold values from 44 to 176, as said below
Outputs:
- block_out: bfloat16 [8, 128, 360, 768], P('dp', 'row')
- input_grad: bfloat16 [8, 128, 360, 768], P('dp', 'row')
- weight_grads: float32 [2, 2, 8, 96, 96], replicated
- bias_grads: float32 [2, 2, 768], replicated
- gain_grad: float32 [768], replicated
The draws below stay inside these ranges and needn't reach their ends.
Inputs may be any that keep to these rules, and one draw needn't show every extreme that they name: `cutoffs`: one cutoff equals 176 and one equals 44.
All inputs are finite; a program needn't handle non-finite values.
Results may differ from the reference program's by a relative error of at most 0.015.
Values may be sent and summed in bfloat16 or wider, within the bound.
No kernel may reach another device: no remote copies, remote signals or barrier semaphores. Data moves between devices by JAX's collectives and lax.ppermute only.
A program may use at most 128 MiB of HBM per device.

```python
import math
import jax
import jax.numpy as jnp
from jax import lax

C = 768
NB = 8
BS = 96
W = 360
KW = 176
H = 128
KH = 16
ENS = 8


def draw_cutoffs(key, part):
    key = jax.random.fold_in(key, 7)
    first_key, second_key, third_key = jax.random.split(key, 3)
    values = jax.random.randint(first_key, (KH,), KW // 4, KW + 1)
    highest = jax.random.randint(second_key, (), 0, KH)
    lowest = jnp.mod(highest + 1 + jax.random.randint(third_key, (), 0, KH - 1), KH)
    positions = jnp.arange(KH, dtype=jnp.int32)
    values = jnp.where(positions == highest, KW, values)
    values = jnp.where(positions == lowest, KW // 4, values)
    return values.astype(jnp.int32)


def steps_of(stream_key, shape, cuts, low, top_value):
    gain = 1.0
    for axis_at, parts in cuts:
        steps = jax.random.uniform(jax.random.fold_in(jax.random.fold_in(stream_key, 6), axis_at), (parts,), jnp.float32, low / len(cuts), top_value / len(cuts))
        gain = gain * jnp.repeat(jnp.exp(steps), shape[axis_at] // parts).reshape((-1,) + (1,) * (len(shape) - 1 - axis_at))
    return gain


def centred(key, extent, width, bound, shards=(), held_as=jnp.bfloat16):
    drawn = width * jax.random.normal(key, extent, jnp.float32)
    if shards:
        drawn = drawn * steps_of(key, extent, shards, -0.22, 0.18)
    return jnp.clip(drawn, -bound, bound).astype(held_as)


def setup_inputs(seed: int = 0) -> dict:
    keys = jax.random.split(jax.random.key(seed), 7)
    fields = centred(keys[0], (ENS, H, W, C), 1.0, 6.0, ((0, 8), (1, 16)))
    cotangent = centred(keys[1], (ENS, H, W, C), 1.0, 6.0, ((0, 8), (1, 16)))
    norm_gain = jnp.clip(1.0 + 0.1 * jax.random.normal(keys[2], (C,), jnp.float32), 0.5, 1.5)
    weights = centred(keys[3], (2, 2, NB, BS, BS), (2 * BS) ** -0.5, 0.4375)
    biases = centred(keys[4], (2, 2, C), 0.5, 3.0, (), jnp.float32)
    cutoffs = draw_cutoffs(jax.random.fold_in(keys[6], 71), 0)
    return {"fields": fields, "cotangent": cotangent, "norm_gain": norm_gain, "weights": weights, "biases": biases, "cutoffs": cutoffs}


norm_eps = 1e-06
gelu_coef = 0.7978845608
cube_coef = 0.044715

def floats(array):
    return array.astype(jnp.float32)

def gelu_pair(values):
    inner = jnp.tanh(gelu_coef * (values + cube_coef * values * values * values))
    value = 0.5 * values * (1.0 + inner)
    slope = 0.5 * (1.0 + inner) + 0.5 * values * (1.0 - inner * inner) * gelu_coef * (1.0 + 3.0 * cube_coef * values * values)
    return (value, slope)

def long_tables(lon_count, wave_count):
    lon_cells = jnp.arange(lon_count, dtype=jnp.int32)
    numbers = jnp.arange(wave_count, dtype=jnp.int32)
    angles = jnp.mod(numbers[:, None] * lon_cells[None, :], lon_count).astype(jnp.float32) * (2.0 * math.pi / lon_count)
    forward = jnp.stack([jnp.cos(angles), -jnp.sin(angles)]) / math.sqrt(lon_count)
    factor = jnp.where(numbers == 0, 1.0, 2.0).astype(jnp.float32)
    inverse = forward * factor[None, :, None]
    return (forward.astype(jnp.bfloat16), inverse.astype(jnp.bfloat16))

def latitude_tables(mode_count, latitudes, lat_count):
    mode_index = jnp.arange(mode_count, dtype=jnp.int32)
    signed = jnp.where(mode_index < mode_count // 2, mode_index, mode_index - mode_count)
    angles = jnp.mod(signed[:, None] * latitudes[None, :], lat_count).astype(jnp.float32) * (2.0 * math.pi / lat_count)
    scaled = 1.0 / math.sqrt(lat_count)
    return ((jnp.cos(angles) * scaled).astype(jnp.bfloat16), (jnp.sin(angles) * scaled).astype(jnp.bfloat16))

def long_forward(field_in, long_table):
    return jnp.einsum('pkw,rwc->prkc', floats(long_table), floats(field_in))

def long_inverse(spectrum, long_table):
    return jnp.einsum('pkw,prkc->rwc', floats(long_table), floats(spectrum))

def lat_forward(cos_table, sin_table, real_part, imag_part):
    cosine, sine_mat = (floats(cos_table), floats(sin_table))
    real_part, imag_part = (floats(real_part), floats(imag_part))
    out_real = jnp.einsum('qh,hkc->qkc', cosine, real_part) + jnp.einsum('qh,hkc->qkc', sine_mat, imag_part)
    out_imag = jnp.einsum('qh,hkc->qkc', cosine, imag_part) - jnp.einsum('qh,hkc->qkc', sine_mat, real_part)
    return (out_real, out_imag)

def lat_inverse(cos_table, sin_table, real_part, imag_part):
    cosine, sine_mat = (floats(cos_table), floats(sin_table))
    real_part, imag_part = (floats(real_part), floats(imag_part))
    out_real = jnp.einsum('qh,qkc->hkc', cosine, real_part) - jnp.einsum('qh,qkc->hkc', sine_mat, imag_part)
    out_imag = jnp.einsum('qh,qkc->hkc', sine_mat, real_part) + jnp.einsum('qh,qkc->hkc', cosine, imag_part)
    return (out_real, out_imag)

def block_product(real_part, imag_part, layer_mats):
    block_count, block_size = (layer_mats.shape[1], layer_mats.shape[2])
    real_part = floats(real_part).reshape(-1, block_count, block_size)
    imag_part = floats(imag_part).reshape(-1, block_count, block_size)
    mat_real, mat_imag = (floats(layer_mats[0]), floats(layer_mats[1]))

    def multiply(operand, matrix):
        return jnp.einsum('mni,nio->mno', operand, matrix)
    out_real = multiply(real_part, mat_real) - multiply(imag_part, mat_imag)
    out_imag = multiply(real_part, mat_imag) + multiply(imag_part, mat_real)
    return (out_real.reshape(-1, block_count * block_size), out_imag.reshape(-1, block_count * block_size))

def block_adjoint(real_part, imag_part, layer_mats):
    block_count, block_size = (layer_mats.shape[1], layer_mats.shape[2])
    real_part = floats(real_part).reshape(-1, block_count, block_size)
    imag_part = floats(imag_part).reshape(-1, block_count, block_size)
    mat_real, mat_imag = (floats(layer_mats[0]), floats(layer_mats[1]))

    def multiply(operand, matrix):
        return jnp.einsum('mno,nio->mni', operand, matrix)
    out_real = multiply(real_part, mat_real) + multiply(imag_part, mat_imag)
    out_imag = multiply(imag_part, mat_real) - multiply(real_part, mat_imag)
    return (out_real.reshape(-1, block_count * block_size), out_imag.reshape(-1, block_count * block_size))

def block_weight_grad(in_real, in_imag, cot_real, cot_imag, block_count):
    block_size = in_real.shape[1] // block_count
    in_real = floats(in_real).reshape(-1, block_count, block_size)
    in_imag = floats(in_imag).reshape(-1, block_count, block_size)
    cot_real = floats(cot_real).reshape(-1, block_count, block_size)
    cot_imag = floats(cot_imag).reshape(-1, block_count, block_size)

    def multiply(operand, matrix):
        return jnp.einsum('mni,mno->nio', operand, matrix)
    grad_real = multiply(in_real, cot_real) + multiply(in_imag, cot_imag)
    grad_imag = multiply(in_real, cot_imag) - multiply(in_imag, cot_real)
    return jnp.stack([grad_real, grad_imag])

def member_pass(field_in, grad_out, norm_gain, weights, biases, kept_mask, tables):
    fwd_long, inv_long, lat_cos, lat_sin = tables
    channels = field_in.shape[-1]
    block_count = weights.shape[2]
    center = floats(field_in)
    average = lax.optimization_barrier(jnp.mean(center, axis=-1, keepdims=True))
    deviation = center - average
    inverse_std = lax.rsqrt(lax.optimization_barrier(jnp.mean(deviation * deviation, axis=-1, keepdims=True)) + norm_eps)
    normal = deviation * inverse_std
    normed = (normal * norm_gain).astype(jnp.bfloat16)
    spectrum = long_forward(normed, fwd_long).astype(jnp.bfloat16)
    lat_real, lat_imag = lat_forward(lat_cos, lat_sin, spectrum[0], spectrum[1])
    spec_shape = lat_real.shape
    kept_rows = jnp.broadcast_to(kept_mask, spec_shape[:-1] + (1,)).reshape(-1, 1)
    in_real = (lat_real * kept_mask).astype(jnp.bfloat16).reshape(-1, channels)
    in_imag = (lat_imag * kept_mask).astype(jnp.bfloat16).reshape(-1, channels)
    lifted_real, lifted_imag = block_product(in_real, in_imag, weights[0])
    lifted_real = lifted_real + biases[0, 0]
    lifted_imag = lifted_imag + biases[0, 1]
    act_real, slope_real = gelu_pair(lifted_real)
    act_imag, slope_imag = gelu_pair(lifted_imag)
    hidden_real = act_real.astype(jnp.bfloat16)
    hidden_imag = act_imag.astype(jnp.bfloat16)
    output_real, output_imag = block_product(hidden_real, hidden_imag, weights[1])
    output_real = output_real + biases[1, 0]
    output_imag = output_imag + biases[1, 1]
    shrunk_real = (output_real * kept_rows).astype(jnp.bfloat16).reshape(spec_shape)
    shrunk_imag = (output_imag * kept_rows).astype(jnp.bfloat16).reshape(spec_shape)
    back_real, back_imag = lat_inverse(lat_cos, lat_sin, shrunk_real, shrunk_imag)
    back_stack = jnp.stack([back_real, back_imag]).astype(jnp.bfloat16)
    block_out = (center + long_inverse(back_stack, inv_long)).astype(jnp.bfloat16)
    cospectrum = long_forward(grad_out, inv_long).astype(jnp.bfloat16)
    grad_real, grad_imag = lat_forward(lat_cos, lat_sin, cospectrum[0], cospectrum[1])
    upper_real = (grad_real * kept_mask).astype(jnp.bfloat16).reshape(-1, channels)
    upper_imag = (grad_imag * kept_mask).astype(jnp.bfloat16).reshape(-1, channels)
    second_grad = block_weight_grad(hidden_real, hidden_imag, upper_real, upper_imag, block_count)
    second_bias = jnp.stack([lax.optimization_barrier(jnp.sum(floats(upper_real), axis=0)), lax.optimization_barrier(jnp.sum(floats(upper_imag), axis=0))])
    middle_real, middle_imag = block_adjoint(upper_real, upper_imag, weights[1])
    lower_real = (middle_real * slope_real).astype(jnp.bfloat16)
    lower_imag = (middle_imag * slope_imag).astype(jnp.bfloat16)
    first_grad = block_weight_grad(in_real, in_imag, lower_real, lower_imag, block_count)
    first_bias = jnp.stack([lax.optimization_barrier(jnp.sum(floats(lower_real), axis=0)), lax.optimization_barrier(jnp.sum(floats(lower_imag), axis=0))])
    bottom_real, bottom_imag = block_adjoint(lower_real, lower_imag, weights[0])
    bottom_real = (bottom_real * kept_rows).astype(jnp.bfloat16).reshape(spec_shape)
    bottom_imag = (bottom_imag * kept_rows).astype(jnp.bfloat16).reshape(spec_shape)
    stack_real, stack_imag = lat_inverse(lat_cos, lat_sin, bottom_real, bottom_imag)
    bottom_stack = jnp.stack([stack_real, stack_imag]).astype(jnp.bfloat16)
    normed_grad = long_inverse(bottom_stack, fwd_long)
    gain_part = lax.optimization_barrier(jnp.sum(normed_grad * normal, axis=(0, 1)))
    scaled = normed_grad * norm_gain
    dfield = inverse_std * (scaled - lax.optimization_barrier(jnp.mean(scaled, axis=-1, keepdims=True)) - normal * lax.optimization_barrier(jnp.mean(scaled * normal, axis=-1, keepdims=True)))
    input_grad = (floats(grad_out) + dfield).astype(jnp.bfloat16)
    return (block_out, input_grad, jnp.stack([first_grad, second_grad]), jnp.stack([first_bias, second_bias]), gain_part)

def reference(fields, cotangent, norm_gain, weights, biases, cutoffs):
    members, lat_count, lon_count, channels = fields.shape
    mode_count = cutoffs.shape[0]
    fwd_long, inv_long = long_tables(lon_count, KW)
    lat_cos, lat_sin = latitude_tables(mode_count, jnp.arange(lat_count, dtype=jnp.int32), lat_count)
    numbers = jnp.arange(KW, dtype=jnp.int32)
    kept_mask = (numbers[None, :] < cutoffs[:, None]).astype(jnp.float32)[:, :, None]
    tables = (fwd_long, inv_long, lat_cos, lat_sin)

    def per_member(member_pair):
        return member_pass(member_pair[0], member_pair[1], norm_gain, weights, biases, kept_mask, tables)
    results = lax.map(per_member, (fields, cotangent))
    spectral_scale = 1.0 / math.sqrt(members * mode_count * KW)
    gain_scale = 1.0 / math.sqrt(members * lat_count * lon_count)
    weight_grads = lax.optimization_barrier(jnp.sum(results[2], axis=0)) * spectral_scale
    bias_grads = lax.optimization_barrier(jnp.sum(results[3], axis=0)) * spectral_scale
    gain_grad = lax.optimization_barrier(jnp.sum(results[4], axis=0)) * gain_scale
    return (results[0], results[1], weight_grads, bias_grads, gain_grad)
```

```python
import functools
import math

import jax
import jax.numpy as jnp
import ml_dtypes
import numpy as np
from jax import lax
from jax.experimental import pallas as pl
from jax.experimental.pallas import tpu as pltpu
from jax.sharding import PartitionSpec as P

C = 768
NB = 8
BS = 96
W = 360
KW = 176
H = 128
KH = 16
ENS = 8

ROWS = 8
WB = 8
COLS = KW // WB // 2
UNITS = COLS * KH
GC = C // 2
GB = NB // 2
AXES = ("dp", "row")

norm_eps = 1e-06
gelu_coef = 0.7978845608
cube_coef = 0.044715
bf16 = jnp.bfloat16
f32 = jnp.float32
VMEM_LIMIT = 48 * 1024 * 1024


def long_tables():
    ids = np.arange(KW).reshape(COLS, 2, WB).transpose(1, 0, 2)
    angle = ((ids[..., None] * np.arange(W)) % W).astype(np.float64) * (2.0 * math.pi / W)
    forward = np.stack([np.cos(angle), -np.sin(angle)], axis=2).astype(np.float32)
    forward = forward / np.float32(math.sqrt(W))
    factor = np.where(ids == 0, 1.0, 2.0).astype(np.float32)[:, :, None, :, None]
    forward, inverse = (
        table.reshape(2, COLS * 2 * WB, W).astype(ml_dtypes.bfloat16)
        for table in (forward, forward * factor)
    )
    return forward, inverse


def latitude_table():
    modes = np.arange(KH)
    signed = np.where(modes < KH // 2, modes, modes - KH)
    angle = ((signed[:, None] * np.arange(H)) % H).astype(np.float64) * (2.0 * math.pi / H)
    cos = (np.cos(angle) / math.sqrt(H)).astype(np.float32).reshape(KH, H // ROWS, ROWS)
    sin = (np.sin(angle) / math.sqrt(H)).astype(np.float32).reshape(KH, H // ROWS, ROWS)
    mixed = np.stack([np.stack([cos, sin], -1), np.stack([-sin, cos], -1)], 1)
    whole = np.einsum("jprhq,kl->rjpkhql", mixed, np.eye(WB, dtype=np.float32))
    return whole.reshape(H // ROWS, KH * 2 * WB, ROWS * 2 * WB).astype(ml_dtypes.bfloat16)


def place(index):
    dp, row = divmod(index, 16)
    y, x_lo = divmod(dp, 2)
    z, rest = divmod(row, 4)
    x_hi, core = divmod(rest, 2)
    return x_hi * 2 + x_lo, y, z, core


def number(x, y, z, core):
    return (y * 2 + x % 2) * 16 + z * 4 + (x // 2) * 2 + core


def shift(array, dx=0, dz=0):
    pairs = []
    for index in range(128):
        x, y, z, core = place(index)
        pairs.append((index, number((x + dx) % 4, y, (z + dz) % 4, core)))
    return lax.ppermute(array, AXES, pairs)


def swap(array, fx=0, fy=0, fz=0, fc=0):
    pairs = []
    for index in range(128):
        x, y, z, core = place(index)
        pairs.append((index, number(x ^ fx, y ^ fy, z ^ fz, core ^ fc)))
    return lax.ppermute(array, AXES, pairs)


def call(kernel, name, grid, in_specs, out_specs, out_shape, scratch=(), flops=0, moved=0):
    return pl.pallas_call(
        kernel,
        name=name,
        grid_spec=pltpu.PrefetchScalarGridSpec(
            num_scalar_prefetch=3,
            grid=grid,
            in_specs=in_specs,
            out_specs=out_specs,
            scratch_shapes=list(scratch),
        ),
        out_shape=out_shape,
        compiler_params=pltpu.CompilerParams(vmem_limit_bytes=VMEM_LIMIT),
        cost_estimate=pl.CostEstimate(flops=flops, bytes_accessed=moved, transcendentals=0),
    )


def layer_norm(block):
    center = block.astype(f32)
    deviation = center - jnp.mean(center, axis=-1, keepdims=True)
    inverse_std = lax.rsqrt(jnp.mean(deviation * deviation, axis=-1, keepdims=True) + norm_eps)
    return deviation * inverse_std, inverse_std


def dot(left, right):
    return jnp.dot(left, right, preferred_element_type=f32)


def dot_nt(left, right):
    return lax.dot_general(left, right, (((1,), (1,)), ((), ())), preferred_element_type=f32)


def dot_tn(left, right):
    return lax.dot_general(left, right, (((0,), (0,)), ((), ())), preferred_element_type=f32)


def own_table(shape):
    return pl.BlockSpec((1,) + shape, lambda i, info, slots, cuts: (info[2], 0, 0))


def beside_table(shape):
    return pl.BlockSpec((1,) + shape, lambda i, info, slots, cuts: (1 - info[2], 0, 0))


def row_block(*shape):
    zeros = (0,) * len(shape)
    return pl.BlockSpec((1,) + shape, lambda i, info, slots, cuts: (i,) + zeros)


def fixed(*shape):
    zeros = (0,) * len(shape)
    return pl.BlockSpec(shape, lambda i, info, slots, cuts: zeros)


def lon_forward(scalars, array, table, gain=None):
    def kernel(info, slots, cuts, own_t, beside_t, x, *rest):
        if gain is None:
            own, beside = rest
            rows = x[0]
        else:
            scale, own, beside = rest
            rows = (layer_norm(x[0])[0] * scale[...]).astype(bf16)
        own[0] = dot(own_t[0], rows).astype(bf16).reshape(COLS, 2 * WB, C)
        beside[0] = dot(beside_t[0], rows).astype(bf16).reshape(COLS, 2 * WB, C)

    specs = [own_table((KW, W)), beside_table((KW, W)), row_block(W, C)]
    operands = [table, table, array]
    if gain is not None:
        specs.append(fixed(1, C))
        operands.append(gain)
    shape = jax.ShapeDtypeStruct((ROWS, COLS, 2 * WB, C), bf16)
    return call(
        kernel,
        "lon_forward",
        (ROWS,),
        specs,
        [row_block(COLS, 2 * WB, C)] * 2,
        [shape, shape],
        flops=2 * ROWS * 2 * KW * W * C,
        moved=2 * ROWS * C * (W + 2 * KW),
    )(*scalars, *operands)


def lane_block(lanes, *shape):
    zeros = (0,) * len(shape)
    return pl.BlockSpec(shape + (lanes,), lambda i, info, slots, cuts: zeros + (i,))


def lat_tables(shape):
    return [
        pl.BlockSpec((1,) + shape, lambda i, info, slots, cuts: (info[3], 0, 0)),
        pl.BlockSpec((1,) + shape, lambda i, info, slots, cuts: (info[4], 0, 0)),
    ]


LANES = 256


def slot_base(info, step, half, owned):
    return (lax.rem(info[0] + step, 4) * 2 + lax.rem(info[1] + half, 2)) * owned


def lat_forward(scalars, own, beside, table, owned):
    def kernel(info, slots, cuts, own_t, beside_t, x_own, x_beside, *rest):
        outs, units = rest[:8], rest[8]
        mix = jnp.concatenate([own_t[0], beside_t[0]], axis=1)
        for col in range(COLS):
            rows = jnp.concatenate(
                [x_own[:, col].reshape(-1, LANES), x_beside[:, col].reshape(-1, LANES)], axis=0
            )
            units[col * KH : (col + 1) * KH] = dot(mix, rows).astype(bf16).reshape(KH, 2 * WB, LANES)
        units[UNITS] = jnp.zeros((2 * WB, LANES), bf16)
        for step in range(4):
            for half in range(2):
                base = slot_base(info, step, half, owned)
                for at in range(owned):
                    outs[step * 2 + half][at] = units[slots[base + at]]

    shape = jax.ShapeDtypeStruct((owned, 2 * WB, C), bf16)
    return call(
        kernel,
        "lat_forward",
        (C // LANES,),
        lat_tables((KH * 2 * WB, ROWS * 2 * WB)) + [lane_block(LANES, ROWS, COLS, 2 * WB)] * 2,
        [lane_block(LANES, owned, 2 * WB)] * 8,
        [shape] * 8,
        [pltpu.VMEM((UNITS + 1, 2 * WB, LANES), bf16)],
        flops=2 * 256 * 256 * C * COLS,
        moved=2 * C * 16 * (UNITS + 8 * owned),
    )(*scalars, table, table, own, beside)


def lat_inverse(scalars, pieces, table, owned):
    def kernel(info, slots, cuts, own_t, beside_t, *rest):
        arrived, (own, beside, units) = rest[:8], rest[8:]
        units[...] = jnp.zeros(units.shape, bf16)
        for step in range(4):
            for half in range(2):
                base = slot_base(info, step, half, owned)
                for at in range(owned):
                    units[slots[base + at]] = arrived[step * 2 + half][at]
        mix = jnp.concatenate([own_t[0], beside_t[0]], axis=0)
        for col in range(COLS):
            rows = dot(mix, units[col * KH : (col + 1) * KH].reshape(-1, LANES)).astype(bf16)
            half = ROWS * 2 * WB
            own[:, col] = rows[:half].reshape(ROWS, 2 * WB, LANES)
            beside[:, col] = rows[half:].reshape(ROWS, 2 * WB, LANES)

    shape = jax.ShapeDtypeStruct((ROWS, COLS, 2 * WB, C), bf16)
    return call(
        kernel,
        "lat_inverse",
        (C // LANES,),
        lat_tables((ROWS * 2 * WB, KH * 2 * WB)) + [lane_block(LANES, owned, 2 * WB)] * 8,
        [lane_block(LANES, ROWS, COLS, 2 * WB)] * 2,
        [shape, shape],
        [pltpu.VMEM((UNITS + 1, 2 * WB, LANES), bf16)],
        flops=2 * 256 * 256 * C * COLS,
        moved=2 * C * 16 * (UNITS + 8 * owned),
    )(*scalars, table, table, *pieces)


def lon_inverse_fields(scalars, own, beside, table, fields):
    def kernel(info, slots, cuts, own_t, beside_t, x_own, x_beside, x, out):
        grid = dot(own_t[0], x_own[0].reshape(KW, C)) + dot(beside_t[0], x_beside[0].reshape(KW, C))
        out[0] = (x[0].astype(f32) + grid).astype(bf16)

    return call(
        kernel,
        "lon_inverse_fields",
        (ROWS,),
        [own_table((W, KW)), beside_table((W, KW))]
        + [row_block(COLS, 2 * WB, C)] * 2
        + [row_block(W, C)],
        row_block(W, C),
        jax.ShapeDtypeStruct((ROWS, W, C), bf16),
        flops=2 * ROWS * 2 * KW * W * C,
        moved=2 * ROWS * C * (2 * W + 2 * KW),
    )(*scalars, table, table, own, beside, fields)


def lon_inverse_grad(scalars, own, beside, table, fields, cotangent, gain):
    def kernel(info, slots, cuts, own_t, beside_t, x_own, x_beside, x, cot, scale, out):
        grid = dot(own_t[0], x_own[0].reshape(KW, C)) + dot(beside_t[0], x_beside[0].reshape(KW, C))
        normal, inverse_std = layer_norm(x[0])
        scaled = grid * scale[...]
        first = jnp.mean(scaled, axis=-1, keepdims=True)
        second = jnp.mean(scaled * normal, axis=-1, keepdims=True)
        grad = inverse_std * (scaled - first - normal * second)
        out[0] = (cot[0].astype(f32) + grad).astype(bf16)

    return call(
        kernel,
        "lon_inverse_grad",
        (ROWS,),
        [own_table((W, KW)), beside_table((W, KW))]
        + [row_block(COLS, 2 * WB, C)] * 2
        + [row_block(W, C)] * 2
        + [fixed(1, C)],
        row_block(W, C),
        jax.ShapeDtypeStruct((ROWS, W, C), bf16),
        flops=2 * ROWS * 2 * KW * W * C,
        moved=2 * ROWS * C * (3 * W + 2 * KW),
    )(*scalars, table, table, own, beside, fields, cotangent, gain)


def wide_weights(scalars, weights):
    def kernel(info, slots, cuts, w, out):
        row = lax.broadcasted_iota(jnp.int32, (BS, GC), 0)
        lane = lax.broadcasted_iota(jnp.int32, (BS, GC), 1)
        for layer in range(2):
            for block in range(GB):
                move = (lane == row + block * BS).astype(f32).astype(bf16)
                real = dot(w[layer, 0, block], move)
                imag = dot(w[layer, 1, block], move)
                top = slice(block * BS, (block + 1) * BS)
                low = slice(GC + block * BS, GC + (block + 1) * BS)
                out[layer, 0, top, :GC] = real.astype(bf16)
                out[layer, 0, top, GC:] = imag.astype(bf16)
                out[layer, 0, low, :GC] = (-imag).astype(bf16)
                out[layer, 0, low, GC:] = real.astype(bf16)

    return call(
        kernel,
        "wide_weights",
        (2,),
        [pl.BlockSpec((2, 2, GB, BS, BS), lambda i, info, slots, cuts: (0, 0, i, 0, 0))],
        pl.BlockSpec((2, 1, C, C), lambda i, info, slots, cuts: (0, i, 0, 0)),
        jax.ShapeDtypeStruct((2, 2, C, C), bf16),
        moved=2 * 5 * C * C,
    )(*scalars, weights)


def gelu_pair(values):
    inner = jnp.tanh(gelu_coef * (values + cube_coef * values * values * values))
    value = 0.5 * values * (1.0 + inner)
    slope = 0.5 * (1.0 + inner) + 0.5 * values * (1.0 - inner * inner) * gelu_coef * (
        1.0 + 3.0 * cube_coef * values * values
    )
    return (value, slope)


def kept_of(info, slots, cuts, at, owned):
    unit = slots[(info[0] * 2 + info[5]) * owned + at]
    first = WB * (2 * lax.div(unit, KH) + info[2])
    return jnp.where(unit < UNITS, cuts[lax.rem(unit, KH)] - first, 0)


def gather_units(info, slots, cuts, left, right, held, owned):
    row = lax.broadcasted_iota(jnp.int32, (WB, GC), 0)
    for at in range(owned):
        unit = left[at].astype(f32) + right[at].astype(f32)
        kept = row < kept_of(info, slots, cuts, at, owned)
        rows = slice(at * WB, (at + 1) * WB)
        held[rows, :GC] = jnp.where(kept, unit[:WB], 0.0)
        held[rows, GC:] = jnp.where(kept, unit[WB:], 0.0)
    return held[...].astype(bf16)


def scatter_units(info, slots, cuts, held, out, owned):
    row = lax.broadcasted_iota(jnp.int32, (WB, GC), 0)
    for at in range(owned):
        kept = row < kept_of(info, slots, cuts, at, owned)
        rows = slice(at * WB, (at + 1) * WB)
        real = jnp.where(kept, held[rows, :GC], 0.0)
        imag = jnp.where(kept, held[rows, GC:], 0.0)
        out[at] = jnp.concatenate([real, imag], axis=0).astype(bf16)


def group_block(rows):
    return pl.BlockSpec((1, rows, C), lambda i, info, slots, cuts: (i, 0, 0))


def weight_block(layer):
    return pl.BlockSpec((1, 1, C, C), lambda i, info, slots, cuts: (layer, i, 0, 0))


def spectral_forward(scalars, left, right, wide, biases, owned):
    count = owned * WB

    def kernel(info, slots, cuts, xl, xr, w0, w1, bias, out, given, hidden, slope, held):
        given[0] = gather_units(info, slots, cuts, xl, xr, held, owned)
        b0 = jnp.concatenate([bias[0, 0:1, :], bias[0, 1:2, :]], axis=1)
        b1 = jnp.concatenate([bias[1, 0:1, :], bias[1, 1:2, :]], axis=1)
        act, slope[0] = gelu_pair(dot(given[0], w0[0, 0]) + b0)
        hidden[0] = act.astype(bf16)
        held[...] = dot(hidden[0], w1[0, 0]) + b1
        scatter_units(info, slots, cuts, held, out, owned)

    return call(
        kernel,
        "spectral_forward",
        (2,),
        [lane_block(GC, owned, 2 * WB)] * 2
        + [weight_block(0), weight_block(1), lane_block(GC, 2, 2)],
        [lane_block(GC, owned, 2 * WB)] + [group_block(count)] * 3,
        [jax.ShapeDtypeStruct((owned, 2 * WB, C), bf16)]
        + [jax.ShapeDtypeStruct((2, count, C), kind) for kind in (bf16, bf16, f32)],
        [pltpu.VMEM((count, C), f32)],
        flops=8 * count * C * C,
        moved=8 * C * C + 20 * count * C,
    )(*scalars, left, right, wide, wide, biases)


def spectral_backward(scalars, left, right, wide, given, slope, owned):
    count = owned * WB

    def kernel(info, slots, cuts, xl, xr, w0, w1, given, slope, out, upper, lower, sums, held):
        upper[0] = gather_units(info, slots, cuts, xl, xr, held, owned)
        sums[0] = jnp.zeros(sums.shape[1:], f32)
        sums[0, 0:1, :] = jnp.sum(upper[0].astype(f32), axis=0, keepdims=True)
        low = (dot_nt(upper[0], w1[0, 0]) * slope[0]).astype(bf16)
        lower[0] = low
        sums[0, 1:2, :] = jnp.sum(low.astype(f32), axis=0, keepdims=True)
        held[...] = dot_nt(low, w0[0, 0])
        scatter_units(info, slots, cuts, held, out, owned)
        sums[0, 2:3, :] = jnp.sum(held[...] * given[0].astype(f32), axis=0, keepdims=True)

    return call(
        kernel,
        "spectral_backward",
        (2,),
        [lane_block(GC, owned, 2 * WB)] * 2
        + [weight_block(0), weight_block(1), group_block(count), group_block(count)],
        [lane_block(GC, owned, 2 * WB)] + [group_block(count)] * 2 + [group_block(8)],
        [jax.ShapeDtypeStruct((owned, 2 * WB, C), bf16)]
        + [jax.ShapeDtypeStruct((2, count, C), bf16)] * 2
        + [jax.ShapeDtypeStruct((2, 8, C), f32)],
        [pltpu.VMEM((count, C), f32)],
        flops=8 * count * C * C,
        moved=8 * C * C + 20 * count * C,
    )(*scalars, left, right, wide, wide, given, slope)


SHARE = 416


def weight_sums(scalars, given, lower, hidden, upper, sums, owned):
    count = owned * WB

    def kernel(info, slots, cuts, u0, y0, u1, y1, small, out):
        lane = lax.div(lax.broadcasted_iota(jnp.int32, (BS, GC), 1), BS)
        for layer, (u, y) in enumerate(((u0, y0), (u1, y1))):
            whole = dot_tn(u[0], y[0])
            real = whole[:GC, :GC] + whole[GC:, GC:]
            imag = whole[:GC, GC:] - whole[GC:, :GC]
            for part, value in enumerate((real, imag)):
                folded = value[:BS]
                for block in range(1, GB):
                    folded = jnp.where(lane == block, value[block * BS : (block + 1) * BS], folded)
                first = (layer * 2 + part) * BS
                out[0, first : first + BS, :] = folded
        out[0, 4 * BS : 4 * BS + 8, :] = small[0, :, :GC]
        out[0, 4 * BS + 8 : 4 * BS + 16, :] = small[0, :, GC:]
        out[0, 4 * BS + 16 :, :] = jnp.zeros((SHARE - 4 * BS - 16, GC), f32)

    return call(
        kernel,
        "weight_sums",
        (2,),
        [group_block(count)] * 4 + [group_block(8)],
        pl.BlockSpec((1, SHARE, GC), lambda i, info, slots, cuts: (i, 0, 0)),
        jax.ShapeDtypeStruct((2, SHARE, GC), f32),
        flops=8 * count * C * C,
        moved=8 * count * C * 2 + 8 * SHARE * GC,
    )(*scalars, given, lower, hidden, upper, sums)


def halves(array, bit):
    size = array.shape[0] // 2
    keep = lax.dynamic_slice_in_dim(array, bit * size, size, 0)
    send = lax.dynamic_slice_in_dim(array, (1 - bit) * size, size, 0)
    return keep, send


def joined(array, other, bit):
    first = jnp.where(bit == 0, array, other)
    second = jnp.where(bit == 0, other, array)
    return jnp.concatenate([first, second], axis=0)


def sum_everywhere(array, core, y):
    steps = [(core, dict(fc=1)), (lax.div(y, 2), dict(fy=2)), (lax.rem(y, 2), dict(fy=1))]
    for bit, flip in steps:
        keep, send = halves(array, bit)
        array = keep + swap(send, **flip)
    for flip in (dict(fz=1), dict(fz=2), dict(fx=1), dict(fx=2)):
        array = array + swap(array, **flip)
    for bit, flip in reversed(steps):
        array = joined(array, swap(array, **flip), bit)
    return array


def add(*arrays):
    total = arrays[0].astype(f32)
    for array in arrays[1:]:
        total = total + array.astype(f32)
    return total.astype(bf16)


def to_owners(parts):
    own_a, own_b, up_a, up_b, far_a, far_b, down_a, down_b = parts
    from_down = shift(far_a, dz=1)
    from_up = shift(far_b, dz=-1)
    near_b = shift(up_b, dz=1)
    near_a = shift(down_a, dz=-1)
    last_a = shift(add(up_a, from_down), dz=1)
    last_b = shift(add(down_b, from_up), dz=-1)
    left = shift(add(own_a, near_a, last_a), dx=1)
    right = shift(add(own_b, near_b, last_b), dx=-1)
    return left, right


def to_rows(result):
    own_a = shift(result, dx=-1)
    own_b = shift(result, dx=1)
    down_a = shift(own_a, dz=1)
    up_b = shift(own_b, dz=-1)
    down_b = shift(own_b, dz=1)
    up_a = shift(own_a, dz=-1)
    far_a = shift(down_a, dz=1)
    far_b = shift(up_b, dz=-1)
    return own_a, own_b, up_a, up_b, far_a, far_b, down_a, down_b


def unit_slots(cutoffs, core, total):
    unit = jnp.arange(UNITS, dtype=jnp.int32)
    first = WB * (2 * (unit // KH) + core)
    kept = (jnp.tile(cutoffs, COLS) > first).astype(jnp.int32)
    rank = jnp.sum(jnp.where(unit[None, :] <= unit[:, None], kept[None, :], 0), axis=1)
    place_of = jnp.arange(total, dtype=jnp.int32)
    return jnp.sum((rank[None, :] <= place_of[:, None]).astype(jnp.int32), axis=1)


def body(fields, cotangent, norm_gain, weights, biases, cutoffs):
    field_in = fields[0]
    grad_out = cotangent[0]
    dp = lax.axis_index("dp").astype(jnp.int32)
    row = lax.axis_index("row").astype(jnp.int32)
    z, x_hi, core = row // 4, (row // 2) % 2, row % 2
    y, x_lo = dp // 2, dp % 2
    x = x_hi * 2 + x_lo
    half_owned = ((x + 3) % 4) // 2
    beside_row = row + 1 - 2 * core
    zero = jnp.zeros((), jnp.int32)
    info = jnp.stack([z, x_hi, core, row, beside_row, half_owned, zero, zero])
    owned = UNITS // 8
    slots = unit_slots(cutoffs, core, 8 * owned)
    scalars = (info, slots, cutoffs)
    fwd_table, inv_table = long_tables()
    fwd_turned = jnp.asarray(fwd_table.transpose(0, 2, 1))
    inv_turned = jnp.asarray(inv_table.transpose(0, 2, 1))
    fwd_table, inv_table = jnp.asarray(fwd_table), jnp.asarray(inv_table)
    lat_np = latitude_table()
    lat_table = jnp.asarray(lat_np)
    lat_turned = jnp.asarray(lat_np.transpose(0, 2, 1))
    gain = norm_gain.reshape(1, C)

    f_own, f_send = lon_forward(scalars, field_in, fwd_table, gain)
    f_recv = swap(f_send, fc=1)
    g_own, g_send = lon_forward(scalars, grad_out, inv_table)
    g_recv = swap(g_send, fc=1)
    f_parts = lat_forward(scalars, f_own, f_recv, lat_table, owned)
    f_left, f_right = to_owners(f_parts)
    g_parts = lat_forward(scalars, g_own, g_recv, lat_table, owned)
    wide = wide_weights(scalars, weights)
    shrunk, given, hidden, slope = spectral_forward(scalars, f_left, f_right, wide, biases, owned)
    g_left, g_right = to_owners(g_parts)
    f_pieces = to_rows(shrunk)
    bottom, upper, lower, sums = spectral_backward(
        scalars, g_left, g_right, wide, given, slope, owned
    )
    g_pieces = to_rows(bottom)
    shares = weight_sums(scalars, given, lower, hidden, upper, sums, owned)
    totals = sum_everywhere(shares.reshape(2 * SHARE, GC), core, y).reshape(2, SHARE, GC)
    f_own, f_send = lat_inverse(scalars, f_pieces, lat_turned, owned)
    f_recv = swap(f_send, fc=1)
    block_out = lon_inverse_fields(scalars, f_own, f_recv, inv_turned, field_in)
    g_own, g_send = lat_inverse(scalars, g_pieces, lat_turned, owned)
    g_recv = swap(g_send, fc=1)
    input_grad = lon_inverse_grad(
        scalars, g_own, g_recv, fwd_turned, field_in, grad_out, gain
    )

    spectral_scale = 1.0 / math.sqrt(ENS * KH * KW)
    gain_scale = 1.0 / math.sqrt(ENS * H * W)
    weight_grads = totals[:, : 4 * BS].reshape(2, 2, 2, BS, GB, BS) * spectral_scale
    weight_grads = weight_grads.transpose(1, 2, 0, 4, 3, 5).reshape(2, 2, NB, BS, BS)
    small = totals[:, 4 * BS : 4 * BS + 16].reshape(2, 2, 8, GC).transpose(2, 1, 0, 3).reshape(8, 2, C)
    bias_grads = jnp.stack([small[1], small[0]]) * spectral_scale
    gain_grad = (small[2, 0] + small[2, 1]) * gain_scale / norm_gain
    return (block_out[None], input_grad[None], weight_grads, bias_grads, gain_grad)


def solution(mesh):
    placed = (P("dp", "row", None, None), P("dp", "row", None, None), P(), P(), P(), P())
    return jax.shard_map(
        body,
        mesh=mesh,
        in_specs=placed,
        out_specs=(P("dp", "row", None, None), P("dp", "row", None, None), P(), P(), P()),
        check_vma=False,
    )
```

```python
import functools
import math

import jax
import jax.numpy as jnp
import ml_dtypes
import numpy as np
from jax import lax
from jax.experimental import pallas as pl
from jax.experimental.pallas import tpu as pltpu
from jax.sharding import PartitionSpec as P

C = 768
NB = 8
BS = 96
W = 360
KW = 176
H = 128
KH = 16
ENS = 8

ROWS = 8
WB = 8
COLS = KW // WB // 2
UNITS = COLS * KH
GC = C // 2
GB = NB // 2
AXES = ("dp", "row")

norm_eps = 1e-06
gelu_coef = 0.7978845608
cube_coef = 0.044715
bf16 = jnp.bfloat16
f32 = jnp.float32
COST = 0
VMEM_LIMIT = 48 * 1024 * 1024
VMEM_MOST = 60 * 1024 * 1024


def first_wave(col, core):
    return WB * (2 * col + (core + col) % 2)


def long_tables():
    firsts = np.array([[first_wave(col, core) for col in range(COLS)] for core in range(2)])
    ids = firsts[:, :, None] + np.arange(WB)
    angle = ((ids[..., None] * np.arange(W)) % W).astype(np.float64) * (2.0 * math.pi / W)
    forward = np.stack([np.cos(angle), -np.sin(angle)], axis=2).astype(np.float32)
    forward = forward / np.float32(math.sqrt(W))
    factor = np.where(ids == 0, 1.0, 2.0).astype(np.float32)[:, :, None, :, None]
    forward, inverse = (
        table.reshape(2, COLS * 2 * WB, W).astype(ml_dtypes.bfloat16)
        for table in (forward, forward * factor)
    )
    return forward, inverse


def latitude_table():
    modes = np.arange(KH)
    signed = np.where(modes < KH // 2, modes, modes - KH)
    angle = ((signed[:, None] * np.arange(H)) % H).astype(np.float64) * (2.0 * math.pi / H)
    cos = (np.cos(angle) / math.sqrt(H)).astype(np.float32).reshape(KH, H // ROWS, ROWS)
    sin = (np.sin(angle) / math.sqrt(H)).astype(np.float32).reshape(KH, H // ROWS, ROWS)
    mixed = np.stack([np.stack([cos, sin], -1), np.stack([-sin, cos], -1)], 1)
    whole = np.einsum("jprhq,kl->rjpkhql", mixed, np.eye(WB, dtype=np.float32))
    return whole.reshape(H // ROWS, KH * 2 * WB, ROWS * 2 * WB).astype(ml_dtypes.bfloat16)


def place(index):
    dp, row = divmod(index, 16)
    y, x_lo = divmod(dp, 2)
    z, rest = divmod(row, 4)
    x_hi, core = divmod(rest, 2)
    return x_hi * 2 + x_lo, y, z, core


def number(x, y, z, core):
    return (y * 2 + x % 2) * 16 + z * 4 + (x // 2) * 2 + core


def shift(array, dx, name):
    pairs = []
    for index in range(128):
        x, y, z, core = place(index)
        pairs.append((index, number((x + dx) % 4, y, z, core)))
    with jax.named_scope(name):
        return lax.ppermute(array, AXES, pairs)


def onward(array, name):
    pairs = []
    for index in range(128):
        x, y, z, core = place(index)
        pairs.append((index, number(x, y, (z + 1 + 2 * core) % 4, core)))
    with jax.named_scope(name):
        return lax.ppermute(array, AXES, pairs)


def swap(array, name, fx=0, fy=0, fz=0, fc=0):
    pairs = []
    for index in range(128):
        x, y, z, core = place(index)
        pairs.append((index, number(x ^ fx, y ^ fy, z ^ fz, core ^ fc)))
    with jax.named_scope(name):
        return lax.ppermute(array, AXES, pairs)


def call(kernel, name, grid, in_specs, out_specs, out_shape, scratch=(), flops=0, moved=0, limit=None):
    return pl.pallas_call(
        kernel,
        name=name,
        grid_spec=pltpu.PrefetchScalarGridSpec(
            num_scalar_prefetch=3,
            grid=grid,
            in_specs=in_specs,
            out_specs=out_specs,
            scratch_shapes=list(scratch),
        ),
        out_shape=out_shape,
        compiler_params=pltpu.CompilerParams(vmem_limit_bytes=limit or VMEM_LIMIT),
        cost_estimate=pl.CostEstimate(flops=COST*flops, bytes_accessed=COST*moved, transcendentals=0),
    )


def layer_norm(block):
    center = block.astype(f32)
    deviation = center - jnp.mean(center, axis=-1, keepdims=True)
    inverse_std = lax.rsqrt(jnp.mean(deviation * deviation, axis=-1, keepdims=True) + norm_eps)
    return deviation * inverse_std, inverse_std


def dot(left, right):
    return jnp.dot(left, right, preferred_element_type=f32)


def dot_nt(left, right):
    return lax.dot_general(left, right, (((1,), (1,)), ((), ())), preferred_element_type=f32)


def dot_tn(left, right):
    return lax.dot_general(left, right, (((0,), (0,)), ((), ())), preferred_element_type=f32)


def own_table(shape):
    return pl.BlockSpec((1,) + shape, lambda i, info, slots, cuts: (info[2], 0, 0))


def beside_table(shape):
    return pl.BlockSpec((1,) + shape, lambda i, info, slots, cuts: (1 - info[2], 0, 0))


def row_block(*shape):
    zeros = (0,) * (len(shape) - 1)
    return pl.BlockSpec(shape, lambda i, info, slots, cuts: (i,) + zeros)


def fixed(*shape):
    zeros = (0,) * len(shape)
    return pl.BlockSpec(shape, lambda i, info, slots, cuts: zeros)


def lon_forward(scalars, array, table, gain=None):
    step = 4

    def kernel(info, slots, cuts, own_t, beside_t, x, *rest):
        for at in range(step):
            if gain is None:
                own, beside = rest
                rows = x[at]
            else:
                scale, own, beside = rest
                rows = (layer_norm(x[at])[0] * scale[...]).astype(bf16)
            own[at] = dot(own_t[0], rows).astype(bf16).reshape(COLS, 2 * WB, C)
            beside[at] = dot(beside_t[0], rows).astype(bf16).reshape(COLS, 2 * WB, C)

    specs = [own_table((KW, W)), beside_table((KW, W)), row_block(step, W, C)]
    operands = [table, table, array]
    if gain is not None:
        specs.append(fixed(1, C))
        operands.append(gain)
    shape = jax.ShapeDtypeStruct((ROWS, COLS, 2 * WB, C), bf16)
    return call(
        kernel,
        "lon_forward",
        (ROWS // step,),
        specs,
        [row_block(step, COLS, 2 * WB, C)] * 2,
        [shape, shape],
        limit=VMEM_MOST,
        flops=2 * ROWS * 2 * KW * W * C,
        moved=2 * ROWS * C * (W + 2 * KW),
    )(*scalars, *operands)


def lane_block(lanes, *shape):
    zeros = (0,) * len(shape)
    return pl.BlockSpec(shape + (lanes,), lambda i, info, slots, cuts: zeros + (i,))


def lat_tables(shape):
    return [
        pl.BlockSpec((1,) + shape, lambda i, info, slots, cuts: (info[3], 0, 0)),
        pl.BlockSpec((1,) + shape, lambda i, info, slots, cuts: (info[4], 0, 0)),
    ]


LANES = 256


def slot_base(info, step, half, owned):
    return (lax.rem(info[0] + step * info[7], 4) * 2 + lax.rem(info[1] + half, 2)) * owned


def lat_forward(scalars, own, beside, table, owned):
    def kernel(info, slots, cuts, own_t, beside_t, x_own, x_beside, *rest):
        outs, over, units = rest[:8], rest[8], rest[9]
        mix = jnp.concatenate([own_t[0], beside_t[0]], axis=1)
        for col in range(COLS):
            rows = jnp.concatenate(
                [x_own[:, col].reshape(-1, LANES), x_beside[:, col].reshape(-1, LANES)], axis=0
            )
            units[col * KH : (col + 1) * KH] = dot(mix, rows).astype(bf16).reshape(KH, 2 * WB, LANES)
        units[UNITS] = jnp.zeros((2 * WB, LANES), bf16)
        for step in range(4):
            for half in range(2):
                base = slot_base(info, step, half, owned)
                for at in range(owned):
                    outs[step * 2 + half][at] = units[slots[base + at]]
        for at in range(UNITS - 8 * owned):
            over[at] = units[slots[8 * owned + at]]

    shape = jax.ShapeDtypeStruct((owned, 2 * WB, C), bf16)
    return call(
        kernel,
        "lat_forward",
        (C // LANES,),
        lat_tables((KH * 2 * WB, ROWS * 2 * WB)) + [lane_block(LANES, ROWS, COLS, 2 * WB)] * 2,
        [lane_block(LANES, owned, 2 * WB)] * 8 + [lane_block(LANES, UNITS - 8 * owned, 2 * WB)],
        [shape] * 8 + [jax.ShapeDtypeStruct((UNITS - 8 * owned, 2 * WB, C), bf16)],
        [pltpu.VMEM((UNITS + 1, 2 * WB, LANES), bf16)],
        limit=VMEM_MOST,
        flops=2 * 256 * 256 * C * COLS,
        moved=2 * C * 16 * (UNITS + 8 * owned),
    )(*scalars, table, table, own, beside)


def lat_inverse(scalars, pieces, over, table, owned):
    def kernel(info, slots, cuts, own_t, beside_t, *rest):
        arrived, (over, own, beside, units) = rest[:8], rest[8:]
        units[...] = jnp.zeros(units.shape, bf16)
        for step in range(4):
            for half in range(2):
                base = slot_base(info, step, half, owned)
                for at in range(owned):
                    units[slots[base + at]] = arrived[step * 2 + half][at]
        for at in range(UNITS - 8 * owned):
            units[slots[8 * owned + at]] = over[at]
        mix = jnp.concatenate([own_t[0], beside_t[0]], axis=0)
        for col in range(COLS):
            rows = dot(mix, units[col * KH : (col + 1) * KH].reshape(-1, LANES)).astype(bf16)
            half = ROWS * 2 * WB
            own[:, col] = rows[:half].reshape(ROWS, 2 * WB, LANES)
            beside[:, col] = rows[half:].reshape(ROWS, 2 * WB, LANES)

    shape = jax.ShapeDtypeStruct((ROWS, COLS, 2 * WB, C), bf16)
    return call(
        kernel,
        "lat_inverse",
        (C // LANES,),
        lat_tables((ROWS * 2 * WB, KH * 2 * WB)) + [lane_block(LANES, owned, 2 * WB)] * 8
        + [lane_block(LANES, UNITS - 8 * owned, 2 * WB)],
        [lane_block(LANES, ROWS, COLS, 2 * WB)] * 2,
        [shape, shape],
        [pltpu.VMEM((UNITS + 1, 2 * WB, LANES), bf16)],
        flops=2 * 256 * 256 * C * COLS,
        moved=2 * C * 16 * (UNITS + 8 * owned),
    )(*scalars, table, table, *pieces, over)


def grid_rows(own_t, beside_t, x_own, x_beside, at):
    own = dot(own_t[0], x_own[at].reshape(KW, C))
    return own + dot(beside_t[0], x_beside[at].reshape(KW, C))


def lon_inverse_fields(scalars, own, beside, table, fields):
    step = 2

    def kernel(info, slots, cuts, own_t, beside_t, x_own, x_beside, x, out):
        for at in range(step):
            grid = grid_rows(own_t, beside_t, x_own, x_beside, at)
            out[at] = (x[at].astype(f32) + grid).astype(bf16)

    return call(
        kernel,
        "lon_inverse_fields",
        (ROWS // step,),
        [own_table((W, KW)), beside_table((W, KW))]
        + [row_block(step, COLS, 2 * WB, C)] * 2
        + [row_block(step, W, C)],
        row_block(step, W, C),
        jax.ShapeDtypeStruct((ROWS, W, C), bf16),
        flops=2 * ROWS * 2 * KW * W * C,
        moved=2 * ROWS * C * (2 * W + 2 * KW),
    )(*scalars, table, table, own, beside, fields)


def lon_inverse_grad(scalars, own, beside, table, fields, cotangent, gain):
    step = 2

    def kernel(info, slots, cuts, own_t, beside_t, x_own, x_beside, x, cot, scale, out):
        for at in range(step):
            grid = grid_rows(own_t, beside_t, x_own, x_beside, at)
            normal, inverse_std = layer_norm(x[at])
            scaled = grid * scale[...]
            first = jnp.mean(scaled, axis=-1, keepdims=True)
            second = jnp.mean(scaled * normal, axis=-1, keepdims=True)
            grad = inverse_std * (scaled - first - normal * second)
            out[at] = (cot[at].astype(f32) + grad).astype(bf16)

    return call(
        kernel,
        "lon_inverse_grad",
        (ROWS // step,),
        [own_table((W, KW)), beside_table((W, KW))]
        + [row_block(step, COLS, 2 * WB, C)] * 2
        + [row_block(step, W, C)] * 2
        + [fixed(1, C)],
        row_block(step, W, C),
        jax.ShapeDtypeStruct((ROWS, W, C), bf16),
        limit=VMEM_MOST,
        flops=2 * ROWS * 2 * KW * W * C,
        moved=2 * ROWS * C * (3 * W + 2 * KW),
    )(*scalars, table, table, own, beside, fields, cotangent, gain)


def wide_weights(scalars, weights):
    def kernel(info, slots, cuts, w, out):
        row = lax.broadcasted_iota(jnp.int32, (BS, GC), 0)
        lane = lax.broadcasted_iota(jnp.int32, (BS, GC), 1)
        for layer in range(2):
            for block in range(GB):
                move = (lane == row + block * BS).astype(f32).astype(bf16)
                real = dot(w[layer, 0, block], move)
                imag = dot(w[layer, 1, block], move)
                top = slice(block * BS, (block + 1) * BS)
                low = slice(GC + block * BS, GC + (block + 1) * BS)
                out[layer, 0, top, :GC] = real.astype(bf16)
                out[layer, 0, top, GC:] = imag.astype(bf16)
                out[layer, 0, low, :GC] = (-imag).astype(bf16)
                out[layer, 0, low, GC:] = real.astype(bf16)

    return call(
        kernel,
        "wide_weights",
        (2,),
        [pl.BlockSpec((2, 2, GB, BS, BS), lambda i, info, slots, cuts: (0, 0, i, 0, 0))],
        pl.BlockSpec((2, 1, C, C), lambda i, info, slots, cuts: (0, i, 0, 0)),
        jax.ShapeDtypeStruct((2, 2, C, C), bf16),
        moved=2 * 5 * C * C,
    )(*scalars, weights)


def gelu_pair(values):
    inner = jnp.tanh(gelu_coef * (values + cube_coef * values * values * values))
    value = 0.5 * values * (1.0 + inner)
    slope = 0.5 * (1.0 + inner) + 0.5 * values * (1.0 - inner * inner) * gelu_coef * (
        1.0 + 3.0 * cube_coef * values * values
    )
    return (value, slope)


def own_first(info, owned):
    return (info[0] * 2 + info[5]) * owned


def kept_of(info, slots, cuts, place):
    unit = slots[place]
    col = lax.div(unit, KH)
    first = WB * (2 * col + lax.rem(info[2] + col, 2))
    return jnp.where(unit < UNITS, cuts[lax.rem(unit, KH)] - first, 0)


def each(count, step):
    if count > 24:
        pl.loop(0, count)(step)
    else:
        for at in range(count):
            step(at)


def unit_rows(at):
    return pl.ds(pl.multiple_of(at * WB, WB) if not isinstance(at, int) else at * WB, WB)


def gather_units(info, slots, cuts, left, right, held, first):
    row = lax.broadcasted_iota(jnp.int32, (WB, GC), 0)

    def step(at):
        unit = left[at].astype(f32)
        if right is not None:
            unit = unit + right[at].astype(f32)
        kept = row < kept_of(info, slots, cuts, first + at)
        held[unit_rows(at), :GC] = jnp.where(kept, unit[:WB], 0.0)
        held[unit_rows(at), GC:] = jnp.where(kept, unit[WB:], 0.0)

    each(left.shape[0], step)
    return held[...].astype(bf16)


def scatter_units(info, slots, cuts, held, out, first):
    row = lax.broadcasted_iota(jnp.int32, (WB, GC), 0)

    def step(at):
        kept = row < kept_of(info, slots, cuts, first + at)
        real = jnp.where(kept, held[unit_rows(at), :GC], 0.0)
        imag = jnp.where(kept, held[unit_rows(at), GC:], 0.0)
        out[at] = jnp.concatenate([real, imag], axis=0).astype(bf16)

    each(out.shape[0], step)


def group_block(rows):
    return pl.BlockSpec((1, rows, C), lambda i, info, slots, cuts: (i, 0, 0))


def weight_block(layer):
    return pl.BlockSpec((1, 1, C, C), lambda i, info, slots, cuts: (layer, i, 0, 0))


def spectral_forward(scalars, units, wide, biases, first=None):
    owned = units[0].shape[0]
    count = owned * WB

    def kernel(info, slots, cuts, xl, *rest):
        xr = rest[0] if len(units) == 2 else None
        w0, w1, bias, out, given, hidden, slope, held = rest[-8:]
        place = own_first(info, owned) if first is None else first
        given[0] = gather_units(info, slots, cuts, xl, xr, held, place)
        b0 = jnp.concatenate([bias[0, 0:1, :], bias[0, 1:2, :]], axis=1)
        b1 = jnp.concatenate([bias[1, 0:1, :], bias[1, 1:2, :]], axis=1)
        act, slope[0] = gelu_pair(dot(given[0], w0[0, 0]) + b0)
        hidden[0] = act.astype(bf16)
        held[...] = dot(hidden[0], w1[0, 0]) + b1
        scatter_units(info, slots, cuts, held, out, place)

    return call(
        kernel,
        "spectral_forward",
        (2,),
        [lane_block(GC, owned, 2 * WB)] * len(units)
        + [weight_block(0), weight_block(1), lane_block(GC, 2, 2)],
        [lane_block(GC, owned, 2 * WB)] + [group_block(count)] * 3,
        [jax.ShapeDtypeStruct((owned, 2 * WB, C), bf16)]
        + [jax.ShapeDtypeStruct((2, count, C), kind) for kind in (bf16, bf16, f32)],
        [pltpu.VMEM((count, C), f32)],
        flops=8 * count * C * C,
        moved=8 * C * C + 20 * count * C,
    )(*scalars, *units, wide, wide, biases)


def spectral_backward(scalars, units, wide, given, slope, first=None):
    owned = units[0].shape[0]
    count = owned * WB

    def kernel(info, slots, cuts, xl, *rest):
        xr = rest[0] if len(units) == 2 else None
        w0, w1, given, slope, out, upper, lower, sums, held = rest[-9:]
        place = own_first(info, owned) if first is None else first
        upper[0] = gather_units(info, slots, cuts, xl, xr, held, place)
        sums[0] = jnp.zeros(sums.shape[1:], f32)
        sums[0, 0:1, :] = jnp.sum(upper[0].astype(f32), axis=0, keepdims=True)
        low = (dot_nt(upper[0], w1[0, 0]) * slope[0]).astype(bf16)
        lower[0] = low
        sums[0, 1:2, :] = jnp.sum(low.astype(f32), axis=0, keepdims=True)
        held[...] = dot_nt(low, w0[0, 0])
        scatter_units(info, slots, cuts, held, out, place)
        sums[0, 2:3, :] = jnp.sum(held[...] * given[0].astype(f32), axis=0, keepdims=True)

    return call(
        kernel,
        "spectral_backward",
        (2,),
        [lane_block(GC, owned, 2 * WB)] * len(units)
        + [weight_block(0), weight_block(1), group_block(count), group_block(count)],
        [lane_block(GC, owned, 2 * WB)] + [group_block(count)] * 2 + [group_block(8)],
        [jax.ShapeDtypeStruct((owned, 2 * WB, C), bf16)]
        + [jax.ShapeDtypeStruct((2, count, C), bf16)] * 2
        + [jax.ShapeDtypeStruct((2, 8, C), f32)],
        [pltpu.VMEM((count, C), f32)],
        flops=8 * count * C * C,
        moved=8 * C * C + 20 * count * C,
    )(*scalars, *units, wide, wide, given, slope)


SHARE = 416
PIECE = SHARE // 4


def weight_sums(scalars, given, lower, hidden, upper, sums, more=None):
    count = given.shape[1]

    def group(rows, lanes=C):
        return pl.BlockSpec(
            (1, rows, lanes), lambda i, info, slots, cuts: (lax.rem(i + 1 + info[2], 2), 0, 0)
        )

    def kernel(info, slots, cuts, u0, y0, u1, y1, small, *rest):
        send, keep, out = rest[-3:]
        lane = lax.div(lax.broadcasted_iota(jnp.int32, (BS, GC), 1), BS)
        for layer, (u, y) in enumerate(((u0, y0), (u1, y1))):
            whole = dot_tn(u[0], y[0])
            real = whole[:GC, :GC] + whole[GC:, GC:]
            imag = whole[:GC, GC:] - whole[GC:, :GC]
            for part, value in enumerate((real, imag)):
                folded = value[:BS]
                for block in range(1, GB):
                    folded = jnp.where(lane == block, value[block * BS : (block + 1) * BS], folded)
                first = (layer * 2 + part) * BS
                out[first : first + BS, :] = folded
        out[4 * BS : 4 * BS + 8, :] = small[0, :, :GC]
        out[4 * BS + 8 : 4 * BS + 16, :] = small[0, :, GC:]
        out[4 * BS + 16 :, :] = jnp.zeros((SHARE - 4 * BS - 16, GC), f32)
        total = out[...]
        if more is not None:
            total = total + rest[0][0]

        @pl.when(pl.program_id(0) == 0)
        def _():
            send[...] = total.astype(send.dtype)

        @pl.when(pl.program_id(0) == 1)
        def _():
            keep[...] = total

    return call(
        kernel,
        "weight_sums",
        (2,),
        [group(count)] * 4 + [group(8)] + ([] if more is None else [group(SHARE, GC)]),
        [fixed(SHARE, GC)] * 2,
        [
            jax.ShapeDtypeStruct((SHARE, GC), f32 if more is None else bf16),
            jax.ShapeDtypeStruct((SHARE, GC), f32),
        ],
        [pltpu.VMEM((SHARE, GC), f32)],
    )(*scalars, given, lower, hidden, upper, sums, *([] if more is None else [more]))


def split_sum(scalars, left, right):
    def kernel(info, slots, cuts, left, right, *outs):
        for far in range(4):
            rows = pl.ds(pl.multiple_of(jnp.bitwise_xor(info[6], far) * PIECE, 8), PIECE)
            outs[far][...] = (left[rows, :] + right[rows, :].astype(f32)).astype(bf16)

    return call(
        kernel,
        "split_sum",
        (1,),
        [fixed(SHARE, GC)] * 2,
        [fixed(PIECE, GC)] * 4,
        [jax.ShapeDtypeStruct((PIECE, GC), bf16)] * 4,
        moved=16 * SHARE * GC,
    )(*scalars, left, right)


def place_sums(scalars, pieces, gain):
    spectral_scale = 1.0 / math.sqrt(ENS * KH * KW)
    gain_scale = 1.0 / math.sqrt(ENS * H * W)

    def kernel(info, slots, cuts, p0, p1, p2, p3, scale, weight_out, bias_out, gain_out, held):
        for far, piece in enumerate((p0, p1, p2, p3)):
            rows = pl.ds(pl.multiple_of(jnp.bitwise_xor(info[6], far) * PIECE, 8), PIECE)
            held[info[2], rows, :] = piece[0].astype(f32)
            held[1 - info[2], rows, :] = piece[1].astype(f32)
        for group in range(2):
            lanes = slice(group * GC, (group + 1) * GC)
            for layer in range(2):
                for part in range(2):
                    first = (layer * 2 + part) * BS
                    value = held[group, first : first + BS, :] * spectral_scale
                    for block in range(GB):
                        weight_out[layer, part, group * GB + block] = value[
                            :, block * BS : (block + 1) * BS
                        ]
                    at = 4 * BS + part * 8 + 1 - layer
                    bias_out[layer, part : part + 1, lanes] = (
                        held[group, at : at + 1, :] * spectral_scale
                    )
            at = 4 * BS + 2
            both = held[group, at : at + 1, :] + held[group, at + 8 : at + 9, :]
            gain_out[:, lanes] = both * gain_scale / scale[:, lanes]

    return call(
        kernel,
        "place_sums",
        (1,),
        [fixed(2, PIECE, GC)] * 4 + [fixed(1, C)],
        [fixed(2, 2, NB, BS, BS), fixed(2, 2, C), fixed(1, C)],
        [
            jax.ShapeDtypeStruct((2, 2, NB, BS, BS), f32),
            jax.ShapeDtypeStruct((2, 2, C), f32),
            jax.ShapeDtypeStruct((1, C), f32),
        ],
        [pltpu.VMEM((2, SHARE, GC), f32)],
        moved=16 * SHARE * GC,
    )(*scalars, *pieces, gain)


def add(*arrays):
    total = arrays[0].astype(f32)
    for array in arrays[1:]:
        total = total + array.astype(f32)
    return total.astype(bf16)


def four(own, first, second, third):
    own, first, second, third = (array.astype(f32) for array in (own, first, second, third))
    return ((own + first) + (second + third)).astype(bf16)


class Order:
    def __init__(self, info, slots, cutoffs):
        self.info, self.rest = info, (slots, cutoffs)

    @property
    def scalars(self):
        return (self.info,) + self.rest

    def ready(self, *arrays):
        return lax.optimization_barrier(arrays + (self.info,))[:-1]

    def wait(self, *arrays):
        *arrays, self.info = lax.optimization_barrier(tuple(arrays) + (self.info,))
        return arrays[0] if len(arrays) == 1 else arrays


def is_kept(cutoffs, core):
    unit = jnp.arange(UNITS, dtype=jnp.int32)
    return (jnp.tile(cutoffs, COLS) > first_wave(unit // KH, core)).astype(jnp.int32)


def unit_slots(cutoffs, core, total):
    unit = jnp.arange(UNITS, dtype=jnp.int32)
    kept = is_kept(cutoffs, core)
    rank = jnp.sum(jnp.where(unit[None, :] <= unit[:, None], kept[None, :], 0), axis=1)
    place_of = jnp.arange(total, dtype=jnp.int32)
    return jnp.sum((rank[None, :] <= place_of[:, None]).astype(jnp.int32), axis=1)


def past_slots(order, owned, f_over, g_over, wide, biases):
    groups = [[2 * at + core for at in range(8)] for core in range(2)]
    f_sum, g_sum = lax.psum(
        (f_over.astype(f32), g_over.astype(f32)), "row", axis_index_groups=groups
    )
    first = 8 * owned
    shrunk, given, hidden, slope = spectral_forward(
        order.scalars, (f_sum,), wide, biases, first
    )
    bottom, upper, lower, sums = spectral_backward(
        order.scalars, (g_sum,), wide, given, slope, first
    )
    other, own = weight_sums(order.scalars, given, lower, hidden, upper, sums)
    counted = (order.info[0] == 0) & (order.info[1] == 0)
    more = jnp.where(order.info[2] == 0, jnp.stack([own, other]), jnp.stack([other, own]))
    return shrunk, bottom, jnp.where(counted, more, 0.0)


def whole_pass(owned, field_in, grad_out, gain, weights, biases, cutoffs):
    dp = lax.axis_index("dp").astype(jnp.int32)
    row = lax.axis_index("row").astype(jnp.int32)
    z, x_hi, core = row // 4, (row // 2) % 2, row % 2
    y, x_lo = dp // 2, dp % 2
    half_owned = ((x_hi * 2 + x_lo + 3) % 4) // 2
    info = jnp.stack([z, x_hi, core, row, row + 1 - 2 * core, half_owned, y, 1 + 2 * core])
    order = Order(info, unit_slots(cutoffs, core, UNITS), cutoffs)
    most = jnp.maximum(jnp.sum(is_kept(cutoffs, 0)), jnp.sum(is_kept(cutoffs, 1)))
    wait, ready = order.wait, order.ready
    fwd_table, inv_table = long_tables()
    fwd_turned = jnp.asarray(fwd_table.transpose(0, 2, 1))
    inv_turned = jnp.asarray(inv_table.transpose(0, 2, 1))
    fwd_table, inv_table = jnp.asarray(fwd_table), jnp.asarray(inv_table)
    lat_np = latitude_table()
    lat_table = jnp.asarray(lat_np)
    lat_turned = jnp.asarray(lat_np.transpose(0, 2, 1))

    f_own, f_send = wait(*lon_forward(order.scalars, field_in, fwd_table, gain))
    f_recv = swap(f_send, "f_pair", fc=1)
    g_own, g_send = wait(*lon_forward(order.scalars, grad_out, inv_table))
    f_recv = wait(f_recv)
    g_recv = swap(*ready(g_send), "g_pair", fc=1)

    f0a, f0b, f1a, f1b, f2a, f2b, f3a, f3b, f_over = wait(
        *lat_forward(order.scalars, f_own, f_recv, lat_table, owned)
    )
    fa, fb = onward(f3a, "f3a"), onward(f3b, "f3b")
    g_recv = wait(g_recv)
    g0a, g0b, g1a, g1b, g2a, g2b, g3a, g3b, g_over = wait(
        *lat_forward(order.scalars, g_own, g_recv, lat_table, owned)
    )
    fa = onward(wait(add(f2a, wait(fa))), "f2a")
    fb = onward(wait(add(f2b, wait(fb))), "f2b")
    wide = wait(wide_weights(order.scalars, weights))
    fa = onward(wait(add(f1a, wait(fa))), "f1a")
    fb = onward(wait(add(f1b, wait(fb))), "f1b")
    left = shift(wait(add(f0a, wait(fa))), 1, "f_left")
    (ga,) = ready(g3a)
    ga = onward(ga, "g3a")
    right = shift(wait(add(f0b, wait(fb))), -1, "f_right")
    (gb,) = ready(g3b)
    gb = onward(gb, "g3b")
    ga = onward(wait(add(g2a, wait(ga))), "g2a")
    left = wait(left)
    right = wait(right)
    gb = onward(wait(add(g2b, wait(gb))), "g2b")

    shrunk, given, hidden, slope = wait(
        *spectral_forward(order.scalars, (left, right), wide, biases)
    )
    f0a, f0b = shift(shrunk, -1, "f_back_a"), shift(shrunk, 1, "f_back_b")
    ga = onward(wait(add(g1a, wait(ga))), "g1a")
    gb = onward(wait(add(g1b, wait(gb))), "g1b")
    f0a = wait(f0a)
    f3a = onward(f0a, "f_from3a")
    f0b = wait(f0b)
    f3b = onward(f0b, "f_from3b")
    left = shift(wait(add(g0a, wait(ga))), 1, "g_left")
    right = shift(wait(add(g0b, wait(gb))), -1, "g_right")
    f3a = wait(f3a)
    f2a = onward(f3a, "f_from2a")
    left = wait(left)
    right = wait(right)
    f3b = wait(f3b)
    f2b = onward(f3b, "f_from2b")
    start = ready(f_over, g_over, jnp.zeros((2, SHARE, GC), f32))
    _, f_over, g_over, more = lax.while_loop(
        lambda held: held[0] > 8 * owned,
        lambda held: (
            jnp.zeros((), jnp.int32),
            *past_slots(order, owned, held[1], held[2], wide, biases),
        ),
        (most, *start),
    )
    f_over, g_over, more = wait(f_over, g_over, more)

    bottom, upper, lower, sums = wait(
        *spectral_backward(order.scalars, (left, right), wide, given, slope)
    )
    g0a, g0b = shift(bottom, -1, "g_back_a"), shift(bottom, 1, "g_back_b")
    f2a = wait(f2a)
    f1a = onward(f2a, "f_from1a")
    f2b = wait(f2b)
    f1b = onward(f2b, "f_from1b")
    send, keep = wait(*weight_sums(order.scalars, given, lower, hidden, upper, sums, more))
    f1a = wait(f1a)
    g0a = wait(g0a)
    g3a = onward(g0a, "g_from3a")
    g0b = wait(g0b)
    g3b = onward(g0b, "g_from3b")
    f1b = wait(f1b)

    arrived = swap(*ready(send), "sum_core", fc=1)
    f_own, f_send = wait(
        *lat_inverse(
            order.scalars, (f0a, f0b, f1a, f1b, f2a, f2b, f3a, f3b), f_over, lat_turned, owned
        )
    )
    f_recv = swap(f_send, "f_pair_back", fc=1)
    g3a = wait(g3a)
    g2a = onward(g3a, "g_from2a")
    g3b = wait(g3b)
    g2b = onward(g3b, "g_from2b")
    arrived = wait(arrived)
    pieces = wait(*split_sum(order.scalars, keep, arrived))
    arrived = [
        swap(piece, "sum_y", fy=far) for far, piece in zip((1, 2, 3), ready(*pieces[1:]))
    ]
    g2a = wait(g2a)
    g1a = onward(g2a, "g_from1a")
    g2b = wait(g2b)
    g1b = onward(g2b, "g_from1b")
    arrived = wait(*arrived)
    total = wait(four(pieces[0], *arrived))
    arrived = [swap(total, "sum_x", fx=far) for far in (1, 2, 3)]
    g1a = wait(g1a)
    g1b = wait(g1b)
    arrived = wait(*arrived)
    total = wait(four(total, *arrived))
    arrived = [swap(total, "sum_z", fz=far) for far in (1, 2, 3)]
    g_own, g_send = wait(
        *lat_inverse(
            order.scalars, (g0a, g0b, g1a, g1b, g2a, g2b, g3a, g3b), g_over, lat_turned, owned
        )
    )
    g_recv = swap(g_send, "g_pair_back", fc=1)
    arrived = wait(*arrived)
    total = wait(four(total, *arrived))
    beside = swap(total, "all_core", fc=1)
    f_recv = wait(f_recv)
    block_out = wait(
        lon_inverse_fields(order.scalars, f_own, f_recv, inv_turned, field_in)
    )
    total = wait(jnp.stack([total, wait(beside)]))
    arrived = [swap(total, "all_y", fy=far) for far in (1, 2, 3)]
    g_recv = wait(g_recv)
    input_grad = wait(
        lon_inverse_grad(order.scalars, g_own, g_recv, fwd_turned, field_in, grad_out, gain)
    )
    arrived = wait(*arrived)
    weight_grads, bias_grads, gain_grad = place_sums(
        order.scalars, (total, *arrived), gain
    )
    return (block_out[None], input_grad[None], weight_grads, bias_grads, gain_grad.reshape(C))


def body(fields, cotangent, norm_gain, weights, biases, cutoffs):
    operands = (fields[0], cotangent[0], norm_gain.reshape(1, C), weights, biases, cutoffs)
    return whole_pass(OWNED, *operands)


OWNED = 16


def solution(mesh):
    placed = (P("dp", "row", None, None), P("dp", "row", None, None), P(), P(), P(), P())
    return jax.shard_map(
        body,
        mesh=mesh,
        in_specs=placed,
        out_specs=(P("dp", "row", None, None), P("dp", "row", None, None), P(), P(), P()),
        check_vma=False,
    )
```

```python
import functools
import math

import jax
import jax.numpy as jnp
import ml_dtypes
import numpy as np
from jax import lax
from jax.experimental import pallas as pl
from jax.experimental.pallas import tpu as pltpu
from jax.sharding import PartitionSpec as P

C = 768
NB = 8
BS = 96
W = 360
KW = 176
H = 128
KH = 16
ENS = 8

ROWS = 8
WB = 8
COLS = KW // WB // 2
UNITS = COLS * KH
GC = C // 2
GB = NB // 2
AXES = ("dp", "row")

norm_eps = 1e-06
gelu_coef = 0.7978845608
cube_coef = 0.044715
bf16 = jnp.bfloat16
f32 = jnp.float32
COST = 0
VMEM_LIMIT = 48 * 1024 * 1024
VMEM_MOST = 60 * 1024 * 1024


def first_wave(col, core):
    return WB * (2 * col + (core + col) % 2)


def long_tables():
    firsts = np.array([[first_wave(col, core) for col in range(COLS)] for core in range(2)])
    ids = firsts[:, :, None] + np.arange(WB)
    angle = ((ids[..., None] * np.arange(W)) % W).astype(np.float64) * (2.0 * math.pi / W)
    forward = np.stack([np.cos(angle), -np.sin(angle)], axis=2).astype(np.float32)
    forward = forward / np.float32(math.sqrt(W))
    factor = np.where(ids == 0, 1.0, 2.0).astype(np.float32)[:, :, None, :, None]
    forward, inverse = (
        table.reshape(2, COLS * 2 * WB, W).astype(ml_dtypes.bfloat16)
        for table in (forward, forward * factor)
    )
    return forward, inverse


def latitude_table():
    modes = np.arange(KH)
    signed = np.where(modes < KH // 2, modes, modes - KH)
    angle = ((signed[:, None] * np.arange(H)) % H).astype(np.float64) * (2.0 * math.pi / H)
    cos = (np.cos(angle) / math.sqrt(H)).astype(np.float32).reshape(KH, H // ROWS, ROWS)
    sin = (np.sin(angle) / math.sqrt(H)).astype(np.float32).reshape(KH, H // ROWS, ROWS)
    mixed = np.stack([np.stack([cos, sin], -1), np.stack([-sin, cos], -1)], 1)
    whole = np.einsum("jprhq,kl->rjpkhql", mixed, np.eye(WB, dtype=np.float32))
    return whole.reshape(H // ROWS, KH * 2 * WB, ROWS * 2 * WB).astype(ml_dtypes.bfloat16)


def place(index):
    dp, row = divmod(index, 16)
    y, x_lo = divmod(dp, 2)
    z, rest = divmod(row, 4)
    x_hi, core = divmod(rest, 2)
    return x_hi * 2 + x_lo, y, z, core


def number(x, y, z, core):
    return (y * 2 + x % 2) * 16 + z * 4 + (x // 2) * 2 + core


def shift(array, dx, name):
    pairs = []
    for index in range(128):
        x, y, z, core = place(index)
        pairs.append((index, number((x + dx) % 4, y, z, core)))
    with jax.named_scope(name):
        return lax.ppermute(array, AXES, pairs)


def onward(array, name):
    pairs = []
    for index in range(128):
        x, y, z, core = place(index)
        pairs.append((index, number(x, y, (z + 1 + 2 * core) % 4, core)))
    with jax.named_scope(name):
        return lax.ppermute(array, AXES, pairs)


def swap(array, name, fx=0, fy=0, fz=0, fc=0):
    pairs = []
    for index in range(128):
        x, y, z, core = place(index)
        pairs.append((index, number(x ^ fx, y ^ fy, z ^ fz, core ^ fc)))
    with jax.named_scope(name):
        return lax.ppermute(array, AXES, pairs)


def call(kernel, name, grid, in_specs, out_specs, out_shape, scratch=(), flops=0, moved=0, limit=None):
    return pl.pallas_call(
        kernel,
        name=name,
        grid_spec=pltpu.PrefetchScalarGridSpec(
            num_scalar_prefetch=3,
            grid=grid,
            in_specs=in_specs,
            out_specs=out_specs,
            scratch_shapes=list(scratch),
        ),
        out_shape=out_shape,
        compiler_params=pltpu.CompilerParams(vmem_limit_bytes=limit or VMEM_LIMIT),
        cost_estimate=pl.CostEstimate(flops=COST*flops, bytes_accessed=COST*moved, transcendentals=0),
    )


def layer_norm(block):
    center = block.astype(f32)
    deviation = center - jnp.mean(center, axis=-1, keepdims=True)
    inverse_std = lax.rsqrt(jnp.mean(deviation * deviation, axis=-1, keepdims=True) + norm_eps)
    return deviation * inverse_std, inverse_std


def dot(left, right):
    return jnp.dot(left, right, preferred_element_type=f32)


def dot_nt(left, right):
    return lax.dot_general(left, right, (((1,), (1,)), ((), ())), preferred_element_type=f32)


def dot_tn(left, right):
    return lax.dot_general(left, right, (((0,), (0,)), ((), ())), preferred_element_type=f32)


def own_table(shape):
    return pl.BlockSpec((1,) + shape, lambda i, info, slots, cuts: (info[2], 0, 0))


def beside_table(shape):
    return pl.BlockSpec((1,) + shape, lambda i, info, slots, cuts: (1 - info[2], 0, 0))


def row_block(*shape):
    zeros = (0,) * (len(shape) - 1)
    return pl.BlockSpec(shape, lambda i, info, slots, cuts: (i,) + zeros)


def fixed(*shape):
    zeros = (0,) * len(shape)
    return pl.BlockSpec(shape, lambda i, info, slots, cuts: zeros)


def lon_forward(scalars, array, table, gain=None):
    step = 4

    def kernel(info, slots, cuts, own_t, beside_t, x, *rest):
        for at in range(step):
            if gain is None:
                own, beside = rest
                rows = x[at]
            else:
                scale, own, beside = rest
                rows = (layer_norm(x[at])[0] * scale[...]).astype(bf16)
            own[at] = dot(own_t[0], rows).astype(bf16).reshape(COLS, 2 * WB, C)
            beside[at] = dot(beside_t[0], rows).astype(bf16).reshape(COLS, 2 * WB, C)

    specs = [own_table((KW, W)), beside_table((KW, W)), row_block(step, W, C)]
    operands = [table, table, array]
    if gain is not None:
        specs.append(fixed(1, C))
        operands.append(gain)
    shape = jax.ShapeDtypeStruct((ROWS, COLS, 2 * WB, C), bf16)
    return call(
        kernel,
        "lon_forward",
        (ROWS // step,),
        specs,
        [row_block(step, COLS, 2 * WB, C)] * 2,
        [shape, shape],
        limit=VMEM_MOST,
        flops=2 * ROWS * 2 * KW * W * C,
        moved=2 * ROWS * C * (W + 2 * KW),
    )(*scalars, *operands)


def lane_block(lanes, *shape):
    zeros = (0,) * len(shape)
    return pl.BlockSpec(shape + (lanes,), lambda i, info, slots, cuts: zeros + (i,))


def lat_tables(shape):
    return [
        pl.BlockSpec((1,) + shape, lambda i, info, slots, cuts: (info[3], 0, 0)),
        pl.BlockSpec((1,) + shape, lambda i, info, slots, cuts: (info[4], 0, 0)),
    ]


LANES = 256


def slot_base(info, step, half, owned):
    return (lax.rem(info[0] + step * info[7], 4) * 2 + lax.rem(info[1] + half, 2)) * owned


def lat_forward(scalars, own, beside, table, owned):
    def kernel(info, slots, cuts, own_t, beside_t, x_own, x_beside, *rest):
        outs, over, units = rest[:8], rest[8], rest[9]
        mix = jnp.concatenate([own_t[0], beside_t[0]], axis=1)
        for col in range(COLS):
            rows = jnp.concatenate(
                [x_own[:, col].reshape(-1, LANES), x_beside[:, col].reshape(-1, LANES)], axis=0
            )
            units[col * KH : (col + 1) * KH] = dot(mix, rows).astype(bf16).reshape(KH, 2 * WB, LANES)
        units[UNITS] = jnp.zeros((2 * WB, LANES), bf16)
        for step in range(4):
            for half in range(2):
                base = slot_base(info, step, half, owned)
                for at in range(owned):
                    outs[step * 2 + half][at] = units[slots[base + at]]

        @pl.when(slots[8 * owned] < UNITS)
        def _():
            for at in range(UNITS - 8 * owned):
                over[at] = units[slots[8 * owned + at]]

    shape = jax.ShapeDtypeStruct((owned, 2 * WB, C), bf16)
    return call(
        kernel,
        "lat_forward",
        (C // LANES,),
        lat_tables((KH * 2 * WB, ROWS * 2 * WB)) + [lane_block(LANES, ROWS, COLS, 2 * WB)] * 2,
        [lane_block(LANES, owned, 2 * WB)] * 8 + [lane_block(LANES, UNITS - 8 * owned, 2 * WB)],
        [shape] * 8 + [jax.ShapeDtypeStruct((UNITS - 8 * owned, 2 * WB, C), bf16)],
        [pltpu.VMEM((UNITS + 1, 2 * WB, LANES), bf16)],
        limit=VMEM_MOST,
        flops=2 * 256 * 256 * C * COLS,
        moved=2 * C * 16 * (UNITS + 8 * owned),
    )(*scalars, table, table, own, beside)


def lat_inverse(scalars, pieces, over, table, owned):
    def kernel(info, slots, cuts, own_t, beside_t, *rest):
        arrived, (over, own, beside, units) = rest[:8], rest[8:]
        units[...] = jnp.zeros(units.shape, bf16)
        for step in range(4):
            for half in range(2):
                base = slot_base(info, step, half, owned)
                for at in range(owned):
                    units[slots[base + at]] = arrived[step * 2 + half][at]

        @pl.when(slots[8 * owned] < UNITS)
        def _():
            for at in range(UNITS - 8 * owned):
                units[slots[8 * owned + at]] = over[at]

        mix = jnp.concatenate([own_t[0], beside_t[0]], axis=0)
        for col in range(COLS):
            rows = dot(mix, units[col * KH : (col + 1) * KH].reshape(-1, LANES)).astype(bf16)
            half = ROWS * 2 * WB
            own[:, col] = rows[:half].reshape(ROWS, 2 * WB, LANES)
            beside[:, col] = rows[half:].reshape(ROWS, 2 * WB, LANES)

    shape = jax.ShapeDtypeStruct((ROWS, COLS, 2 * WB, C), bf16)
    return call(
        kernel,
        "lat_inverse",
        (C // LANES,),
        lat_tables((ROWS * 2 * WB, KH * 2 * WB)) + [lane_block(LANES, owned, 2 * WB)] * 8
        + [lane_block(LANES, UNITS - 8 * owned, 2 * WB)],
        [lane_block(LANES, ROWS, COLS, 2 * WB)] * 2,
        [shape, shape],
        [pltpu.VMEM((UNITS + 1, 2 * WB, LANES), bf16)],
        flops=2 * 256 * 256 * C * COLS,
        moved=2 * C * 16 * (UNITS + 8 * owned),
    )(*scalars, table, table, *pieces, over)


def grid_rows(own_t, beside_t, x_own, x_beside, at):
    own = dot(own_t[0], x_own[at].reshape(KW, C))
    return own + dot(beside_t[0], x_beside[at].reshape(KW, C))


def lon_inverse_fields(scalars, own, beside, table, fields):
    step = 2

    def kernel(info, slots, cuts, own_t, beside_t, x_own, x_beside, x, out):
        for at in range(step):
            grid = grid_rows(own_t, beside_t, x_own, x_beside, at)
            out[at] = (x[at].astype(f32) + grid).astype(bf16)

    return call(
        kernel,
        "lon_inverse_fields",
        (ROWS // step,),
        [own_table((W, KW)), beside_table((W, KW))]
        + [row_block(step, COLS, 2 * WB, C)] * 2
        + [row_block(step, W, C)],
        row_block(step, W, C),
        jax.ShapeDtypeStruct((ROWS, W, C), bf16),
        flops=2 * ROWS * 2 * KW * W * C,
        moved=2 * ROWS * C * (2 * W + 2 * KW),
    )(*scalars, table, table, own, beside, fields)


def lon_inverse_grad(scalars, own, beside, table, fields, cotangent, gain):
    step = 2

    def kernel(info, slots, cuts, own_t, beside_t, x_own, x_beside, x, cot, scale, out):
        for at in range(step):
            grid = grid_rows(own_t, beside_t, x_own, x_beside, at)
            normal, inverse_std = layer_norm(x[at])
            scaled = grid * scale[...]
            first = jnp.mean(scaled, axis=-1, keepdims=True)
            second = jnp.mean(scaled * normal, axis=-1, keepdims=True)
            grad = inverse_std * (scaled - first - normal * second)
            out[at] = (cot[at].astype(f32) + grad).astype(bf16)

    return call(
        kernel,
        "lon_inverse_grad",
        (ROWS // step,),
        [own_table((W, KW)), beside_table((W, KW))]
        + [row_block(step, COLS, 2 * WB, C)] * 2
        + [row_block(step, W, C)] * 2
        + [fixed(1, C)],
        row_block(step, W, C),
        jax.ShapeDtypeStruct((ROWS, W, C), bf16),
        limit=VMEM_MOST,
        flops=2 * ROWS * 2 * KW * W * C,
        moved=2 * ROWS * C * (3 * W + 2 * KW),
    )(*scalars, table, table, own, beside, fields, cotangent, gain)


def wide_weights(scalars, weights):
    def kernel(info, slots, cuts, w, out):
        row = lax.broadcasted_iota(jnp.int32, (BS, GC), 0)
        lane = lax.broadcasted_iota(jnp.int32, (BS, GC), 1)
        for layer in range(2):
            for block in range(GB):
                move = (lane == row + block * BS).astype(f32).astype(bf16)
                real = dot(w[layer, 0, block], move)
                imag = dot(w[layer, 1, block], move)
                top = slice(block * BS, (block + 1) * BS)
                low = slice(GC + block * BS, GC + (block + 1) * BS)
                out[layer, 0, top, :GC] = real.astype(bf16)
                out[layer, 0, top, GC:] = imag.astype(bf16)
                out[layer, 0, low, :GC] = (-imag).astype(bf16)
                out[layer, 0, low, GC:] = real.astype(bf16)

    return call(
        kernel,
        "wide_weights",
        (2,),
        [pl.BlockSpec((2, 2, GB, BS, BS), lambda i, info, slots, cuts: (0, 0, i, 0, 0))],
        pl.BlockSpec((2, 1, C, C), lambda i, info, slots, cuts: (0, i, 0, 0)),
        jax.ShapeDtypeStruct((2, 2, C, C), bf16),
        moved=2 * 5 * C * C,
    )(*scalars, weights)


def gelu_pair(values):
    inner = jnp.tanh(gelu_coef * (values + cube_coef * values * values * values))
    value = 0.5 * values * (1.0 + inner)
    slope = 0.5 * (1.0 + inner) + 0.5 * values * (1.0 - inner * inner) * gelu_coef * (
        1.0 + 3.0 * cube_coef * values * values
    )
    return (value, slope)


def own_first(info, owned):
    return (info[0] * 2 + info[5]) * owned


def kept_of(info, slots, cuts, place):
    unit = slots[place]
    col = lax.div(unit, KH)
    first = WB * (2 * col + lax.rem(info[2] + col, 2))
    return jnp.where(unit < UNITS, cuts[lax.rem(unit, KH)] - first, 0)


def each(count, step):
    if count > 24:
        pl.loop(0, count)(step)
    else:
        for at in range(count):
            step(at)


def unit_rows(at):
    return pl.ds(pl.multiple_of(at * WB, WB) if not isinstance(at, int) else at * WB, WB)


def gather_units(info, slots, cuts, left, right, held, first):
    row = lax.broadcasted_iota(jnp.int32, (WB, GC), 0)

    def step(at):
        unit = left[at].astype(f32)
        if right is not None:
            unit = unit + right[at].astype(f32)
        kept = row < kept_of(info, slots, cuts, first + at)
        held[unit_rows(at), :GC] = jnp.where(kept, unit[:WB], 0.0)
        held[unit_rows(at), GC:] = jnp.where(kept, unit[WB:], 0.0)

    each(left.shape[0], step)
    return held[...].astype(bf16)


def scatter_units(info, slots, cuts, held, out, first):
    row = lax.broadcasted_iota(jnp.int32, (WB, GC), 0)

    def step(at):
        kept = row < kept_of(info, slots, cuts, first + at)
        real = jnp.where(kept, held[unit_rows(at), :GC], 0.0)
        imag = jnp.where(kept, held[unit_rows(at), GC:], 0.0)
        out[at] = jnp.concatenate([real, imag], axis=0).astype(bf16)

    each(out.shape[0], step)


def group_block(rows):
    return pl.BlockSpec((1, rows, C), lambda i, info, slots, cuts: (i, 0, 0))


def weight_block(layer):
    return pl.BlockSpec((1, 1, C, C), lambda i, info, slots, cuts: (layer, i, 0, 0))


def spectral_forward(scalars, units, wide, biases, first=None):
    owned = units[0].shape[0]
    count = owned * WB

    def kernel(info, slots, cuts, xl, *rest):
        xr = rest[0] if len(units) == 2 else None
        w0, w1, bias, out, given, hidden, slope, held = rest[-8:]
        place = own_first(info, owned) if first is None else first
        given[0] = gather_units(info, slots, cuts, xl, xr, held, place)
        b0 = jnp.concatenate([bias[0, 0:1, :], bias[0, 1:2, :]], axis=1)
        b1 = jnp.concatenate([bias[1, 0:1, :], bias[1, 1:2, :]], axis=1)
        act, slope[0] = gelu_pair(dot(given[0], w0[0, 0]) + b0)
        hidden[0] = act.astype(bf16)
        held[...] = dot(hidden[0], w1[0, 0]) + b1
        scatter_units(info, slots, cuts, held, out, place)

    return call(
        kernel,
        "spectral_forward",
        (2,),
        [lane_block(GC, owned, 2 * WB)] * len(units)
        + [weight_block(0), weight_block(1), lane_block(GC, 2, 2)],
        [lane_block(GC, owned, 2 * WB)] + [group_block(count)] * 3,
        [jax.ShapeDtypeStruct((owned, 2 * WB, C), bf16)]
        + [jax.ShapeDtypeStruct((2, count, C), kind) for kind in (bf16, bf16, f32)],
        [pltpu.VMEM((count, C), f32)],
        flops=8 * count * C * C,
        moved=8 * C * C + 20 * count * C,
    )(*scalars, *units, wide, wide, biases)


def spectral_backward(scalars, units, wide, given, slope, first=None):
    owned = units[0].shape[0]
    count = owned * WB

    def kernel(info, slots, cuts, xl, *rest):
        xr = rest[0] if len(units) == 2 else None
        w0, w1, given, slope, out, upper, lower, sums, held = rest[-9:]
        place = own_first(info, owned) if first is None else first
        upper[0] = gather_units(info, slots, cuts, xl, xr, held, place)
        sums[0] = jnp.zeros(sums.shape[1:], f32)
        sums[0, 0:1, :] = jnp.sum(upper[0].astype(f32), axis=0, keepdims=True)
        low = (dot_nt(upper[0], w1[0, 0]) * slope[0]).astype(bf16)
        lower[0] = low
        sums[0, 1:2, :] = jnp.sum(low.astype(f32), axis=0, keepdims=True)
        held[...] = dot_nt(low, w0[0, 0])
        scatter_units(info, slots, cuts, held, out, place)
        sums[0, 2:3, :] = jnp.sum(held[...] * given[0].astype(f32), axis=0, keepdims=True)

    return call(
        kernel,
        "spectral_backward",
        (2,),
        [lane_block(GC, owned, 2 * WB)] * len(units)
        + [weight_block(0), weight_block(1), group_block(count), group_block(count)],
        [lane_block(GC, owned, 2 * WB)] + [group_block(count)] * 2 + [group_block(8)],
        [jax.ShapeDtypeStruct((owned, 2 * WB, C), bf16)]
        + [jax.ShapeDtypeStruct((2, count, C), bf16)] * 2
        + [jax.ShapeDtypeStruct((2, 8, C), f32)],
        [pltpu.VMEM((count, C), f32)],
        flops=8 * count * C * C,
        moved=8 * C * C + 20 * count * C,
    )(*scalars, *units, wide, wide, given, slope)


SHARE = 416
PIECE = SHARE // 4


def weight_sums(scalars, given, lower, hidden, upper, sums, more=None):
    count = given.shape[1]

    def group(rows, lanes=C):
        return pl.BlockSpec(
            (1, rows, lanes), lambda i, info, slots, cuts: (lax.rem(i + 1 + info[2], 2), 0, 0)
        )

    def kernel(info, slots, cuts, u0, y0, u1, y1, small, *rest):
        send, keep, out = rest[-3:]
        lane = lax.div(lax.broadcasted_iota(jnp.int32, (BS, GC), 1), BS)
        for layer, (u, y) in enumerate(((u0, y0), (u1, y1))):
            whole = dot_tn(u[0], y[0])
            real = whole[:GC, :GC] + whole[GC:, GC:]
            imag = whole[:GC, GC:] - whole[GC:, :GC]
            for part, value in enumerate((real, imag)):
                folded = value[:BS]
                for block in range(1, GB):
                    folded = jnp.where(lane == block, value[block * BS : (block + 1) * BS], folded)
                first = (layer * 2 + part) * BS
                out[first : first + BS, :] = folded
        out[4 * BS : 4 * BS + 8, :] = small[0, :, :GC]
        out[4 * BS + 8 : 4 * BS + 16, :] = small[0, :, GC:]
        out[4 * BS + 16 :, :] = jnp.zeros((SHARE - 4 * BS - 16, GC), f32)
        total = out[...]
        if more is not None:
            total = total + rest[0][0]

        @pl.when(pl.program_id(0) == 0)
        def _():
            send[...] = total.astype(send.dtype)

        @pl.when(pl.program_id(0) == 1)
        def _():
            keep[...] = total

    return call(
        kernel,
        "weight_sums",
        (2,),
        [group(count)] * 4 + [group(8)] + ([] if more is None else [group(SHARE, GC)]),
        [fixed(SHARE, GC)] * 2,
        [
            jax.ShapeDtypeStruct((SHARE, GC), f32 if more is None else bf16),
            jax.ShapeDtypeStruct((SHARE, GC), f32),
        ],
        [pltpu.VMEM((SHARE, GC), f32)],
    )(*scalars, given, lower, hidden, upper, sums, *([] if more is None else [more]))


def split_sum(scalars, left, right):
    def kernel(info, slots, cuts, left, right, *outs):
        for far in range(4):
            rows = pl.ds(pl.multiple_of(jnp.bitwise_xor(info[6], far) * PIECE, 8), PIECE)
            outs[far][...] = (left[rows, :] + right[rows, :].astype(f32)).astype(bf16)

    return call(
        kernel,
        "split_sum",
        (1,),
        [fixed(SHARE, GC)] * 2,
        [fixed(PIECE, GC)] * 4,
        [jax.ShapeDtypeStruct((PIECE, GC), bf16)] * 4,
        moved=16 * SHARE * GC,
    )(*scalars, left, right)


def place_sums(scalars, pieces, gain):
    spectral_scale = 1.0 / math.sqrt(ENS * KH * KW)
    gain_scale = 1.0 / math.sqrt(ENS * H * W)

    def kernel(info, slots, cuts, p0, p1, p2, p3, scale, weight_out, bias_out, gain_out, held):
        for far, piece in enumerate((p0, p1, p2, p3)):
            rows = pl.ds(pl.multiple_of(jnp.bitwise_xor(info[6], far) * PIECE, 8), PIECE)
            held[info[2], rows, :] = piece[0].astype(f32)
            held[1 - info[2], rows, :] = piece[1].astype(f32)
        for group in range(2):
            lanes = slice(group * GC, (group + 1) * GC)
            for layer in range(2):
                for part in range(2):
                    first = (layer * 2 + part) * BS
                    value = held[group, first : first + BS, :] * spectral_scale
                    for block in range(GB):
                        weight_out[layer, part, group * GB + block] = value[
                            :, block * BS : (block + 1) * BS
                        ]
                    at = 4 * BS + part * 8 + 1 - layer
                    bias_out[layer, part : part + 1, lanes] = (
                        held[group, at : at + 1, :] * spectral_scale
                    )
            at = 4 * BS + 2
            both = held[group, at : at + 1, :] + held[group, at + 8 : at + 9, :]
            gain_out[:, lanes] = both * gain_scale / scale[:, lanes]

    return call(
        kernel,
        "place_sums",
        (1,),
        [fixed(2, PIECE, GC)] * 4 + [fixed(1, C)],
        [fixed(2, 2, NB, BS, BS), fixed(2, 2, C), fixed(1, C)],
        [
            jax.ShapeDtypeStruct((2, 2, NB, BS, BS), f32),
            jax.ShapeDtypeStruct((2, 2, C), f32),
            jax.ShapeDtypeStruct((1, C), f32),
        ],
        [pltpu.VMEM((2, SHARE, GC), f32)],
        moved=16 * SHARE * GC,
    )(*scalars, *pieces, gain)


def add(*arrays):
    total = arrays[0].astype(f32)
    for array in arrays[1:]:
        total = total + array.astype(f32)
    return total.astype(bf16)


def four(own, first, second, third):
    own, first, second, third = (array.astype(f32) for array in (own, first, second, third))
    return ((own + first) + (second + third)).astype(bf16)


class Order:
    def __init__(self, info, slots, cutoffs):
        self.info, self.rest = info, (slots, cutoffs)

    @property
    def scalars(self):
        return (self.info,) + self.rest

    def ready(self, *arrays):
        return lax.optimization_barrier(arrays + (self.info,))[:-1]

    def wait(self, *arrays):
        *arrays, self.info = lax.optimization_barrier(tuple(arrays) + (self.info,))
        return arrays[0] if len(arrays) == 1 else arrays


def is_kept(cutoffs, core):
    unit = jnp.arange(UNITS, dtype=jnp.int32)
    return (jnp.tile(cutoffs, COLS) > first_wave(unit // KH, core)).astype(jnp.int32)


def unit_slots(cutoffs, core, total):
    unit = jnp.arange(UNITS, dtype=jnp.int32)
    kept = is_kept(cutoffs, core)
    rank = jnp.sum(jnp.where(unit[None, :] <= unit[:, None], kept[None, :], 0), axis=1)
    place_of = jnp.arange(total, dtype=jnp.int32)
    return jnp.sum((rank[None, :] <= place_of[:, None]).astype(jnp.int32), axis=1)


def past_slots(order, owned, f_over, g_over, wide, biases):
    groups = [[2 * at + core for at in range(8)] for core in range(2)]
    f_sum, g_sum = lax.psum(
        (f_over.astype(f32), g_over.astype(f32)), "row", axis_index_groups=groups
    )
    first = 8 * owned
    shrunk, given, hidden, slope = spectral_forward(
        order.scalars, (f_sum,), wide, biases, first
    )
    bottom, upper, lower, sums = spectral_backward(
        order.scalars, (g_sum,), wide, given, slope, first
    )
    other, own = weight_sums(order.scalars, given, lower, hidden, upper, sums)
    counted = (order.info[0] == 0) & (order.info[1] == 0)
    more = jnp.where(order.info[2] == 0, jnp.stack([own, other]), jnp.stack([other, own]))
    return shrunk, bottom, jnp.where(counted, more, 0.0)


def whole_pass(owned, field_in, grad_out, gain, weights, biases, cutoffs):
    dp = lax.axis_index("dp").astype(jnp.int32)
    row = lax.axis_index("row").astype(jnp.int32)
    z, x_hi, core = row // 4, (row // 2) % 2, row % 2
    y, x_lo = dp // 2, dp % 2
    half_owned = ((x_hi * 2 + x_lo + 3) % 4) // 2
    info = jnp.stack([z, x_hi, core, row, row + 1 - 2 * core, half_owned, y, 1 + 2 * core])
    order = Order(info, unit_slots(cutoffs, core, UNITS), cutoffs)
    most = jnp.maximum(jnp.sum(is_kept(cutoffs, 0)), jnp.sum(is_kept(cutoffs, 1)))
    wait, ready = order.wait, order.ready
    fwd_table, inv_table = long_tables()
    fwd_turned = jnp.asarray(fwd_table.transpose(0, 2, 1))
    inv_turned = jnp.asarray(inv_table.transpose(0, 2, 1))
    fwd_table, inv_table = jnp.asarray(fwd_table), jnp.asarray(inv_table)
    lat_np = latitude_table()
    lat_table = jnp.asarray(lat_np)
    lat_turned = jnp.asarray(lat_np.transpose(0, 2, 1))

    f_own, f_send = wait(*lon_forward(order.scalars, field_in, fwd_table, gain))
    f_recv = swap(f_send, "f_pair", fc=1)
    g_own, g_send = wait(*lon_forward(order.scalars, grad_out, inv_table))
    f_recv = wait(f_recv)
    g_recv = swap(*ready(g_send), "g_pair", fc=1)

    f0a, f0b, f1a, f1b, f2a, f2b, f3a, f3b, f_over = wait(
        *lat_forward(order.scalars, f_own, f_recv, lat_table, owned)
    )
    fa, fb = onward(f3a, "f3a"), onward(f3b, "f3b")
    g_recv = wait(g_recv)
    g0a, g0b, g1a, g1b, g2a, g2b, g3a, g3b, g_over = wait(
        *lat_forward(order.scalars, g_own, g_recv, lat_table, owned)
    )
    fa = onward(wait(add(f2a, wait(fa))), "f2a")
    fb = onward(wait(add(f2b, wait(fb))), "f2b")
    wide = wait(wide_weights(order.scalars, weights))
    fa = onward(wait(add(f1a, wait(fa))), "f1a")
    fb = onward(wait(add(f1b, wait(fb))), "f1b")
    left = shift(wait(add(f0a, wait(fa))), 1, "f_left")
    (ga,) = ready(g3a)
    ga = onward(ga, "g3a")
    right = shift(wait(add(f0b, wait(fb))), -1, "f_right")
    (gb,) = ready(g3b)
    gb = onward(gb, "g3b")
    ga = onward(wait(add(g2a, wait(ga))), "g2a")
    left = wait(left)
    right = wait(right)
    gb = onward(wait(add(g2b, wait(gb))), "g2b")

    shrunk, given, hidden, slope = wait(
        *spectral_forward(order.scalars, (left, right), wide, biases)
    )
    f0a, f0b = shift(shrunk, -1, "f_back_a"), shift(shrunk, 1, "f_back_b")
    ga = onward(wait(add(g1a, wait(ga))), "g1a")
    gb = onward(wait(add(g1b, wait(gb))), "g1b")
    f0a = wait(f0a)
    f3a = onward(f0a, "f_from3a")
    f0b = wait(f0b)
    f3b = onward(f0b, "f_from3b")
    left = shift(wait(add(g0a, wait(ga))), 1, "g_left")
    right = shift(wait(add(g0b, wait(gb))), -1, "g_right")
    f3a = wait(f3a)
    f2a = onward(f3a, "f_from2a")
    left = wait(left)
    right = wait(right)
    f3b = wait(f3b)
    f2b = onward(f3b, "f_from2b")
    start = ready(f_over, g_over, jnp.zeros((2, SHARE, GC), f32))
    _, f_over, g_over, more = lax.while_loop(
        lambda held: held[0] > 8 * owned,
        lambda held: (
            jnp.zeros((), jnp.int32),
            *past_slots(order, owned, held[1], held[2], wide, biases),
        ),
        (most, *start),
    )
    f_over, g_over, more = wait(f_over, g_over, more)

    bottom, upper, lower, sums = wait(
        *spectral_backward(order.scalars, (left, right), wide, given, slope)
    )
    g0a, g0b = shift(bottom, -1, "g_back_a"), shift(bottom, 1, "g_back_b")
    f2a = wait(f2a)
    f1a = onward(f2a, "f_from1a")
    f2b = wait(f2b)
    f1b = onward(f2b, "f_from1b")
    send, keep = wait(*weight_sums(order.scalars, given, lower, hidden, upper, sums, more))
    f1a = wait(f1a)
    g0a = wait(g0a)
    g3a = onward(g0a, "g_from3a")
    g0b = wait(g0b)
    g3b = onward(g0b, "g_from3b")
    f1b = wait(f1b)

    arrived = swap(*ready(send), "sum_core", fc=1)
    f_own, f_send = wait(
        *lat_inverse(
            order.scalars, (f0a, f0b, f1a, f1b, f2a, f2b, f3a, f3b), f_over, lat_turned, owned
        )
    )
    f_recv = swap(f_send, "f_pair_back", fc=1)
    g3a = wait(g3a)
    g2a = onward(g3a, "g_from2a")
    g3b = wait(g3b)
    g2b = onward(g3b, "g_from2b")
    arrived = wait(arrived)
    pieces = wait(*split_sum(order.scalars, keep, arrived))
    arrived = [
        swap(piece, "sum_y", fy=far) for far, piece in zip((1, 2, 3), ready(*pieces[1:]))
    ]
    g2a = wait(g2a)
    g1a = onward(g2a, "g_from1a")
    g2b = wait(g2b)
    g1b = onward(g2b, "g_from1b")
    arrived = wait(*arrived)
    total = wait(four(pieces[0], *arrived))
    beside = swap(total, "sum_x1", fx=1)
    g1a = wait(g1a)
    total = wait(add(total, wait(beside)))
    beside = swap(total, "sum_x2", fx=2)
    g1b = wait(g1b)
    total = wait(add(total, wait(beside)))
    beside = swap(total, "sum_z1", fz=1)
    g_own, g_send = wait(
        *lat_inverse(
            order.scalars, (g0a, g0b, g1a, g1b, g2a, g2b, g3a, g3b), g_over, lat_turned, owned
        )
    )
    g_recv = swap(g_send, "g_pair_back", fc=1)
    total = wait(add(total, wait(beside)))
    beside = swap(total, "sum_z2", fz=2)
    f_recv = wait(f_recv)
    block_out = wait(
        lon_inverse_fields(order.scalars, f_own, f_recv, inv_turned, field_in)
    )
    total = wait(add(total, wait(beside)))
    total = wait(jnp.stack([total, wait(swap(total, "all_core", fc=1))]))
    arrived = [swap(total, "all_y", fy=far) for far in (1, 2, 3)]
    g_recv = wait(g_recv)
    input_grad = wait(
        lon_inverse_grad(order.scalars, g_own, g_recv, fwd_turned, field_in, grad_out, gain)
    )
    arrived = wait(*arrived)
    weight_grads, bias_grads, gain_grad = place_sums(
        order.scalars, (total, *arrived), gain
    )
    return (block_out[None], input_grad[None], weight_grads, bias_grads, gain_grad.reshape(C))


def body(fields, cotangent, norm_gain, weights, biases, cutoffs):
    operands = (fields[0], cotangent[0], norm_gain.reshape(1, C), weights, biases, cutoffs)
    return whole_pass(OWNED, *operands)


OWNED = 16


def solution(mesh):
    placed = (P("dp", "row", None, None), P("dp", "row", None, None), P(), P(), P(), P())
    return jax.shard_map(
        body,
        mesh=mesh,
        in_specs=placed,
        out_specs=(P("dp", "row", None, None), P("dp", "row", None, None), P(), P(), P()),
        check_vma=False,
    )
```

```python
import functools
import math

import jax
import jax.numpy as jnp
import ml_dtypes
import numpy as np
from jax import lax
from jax.experimental import pallas as pl
from jax.experimental.pallas import tpu as pltpu
from jax.sharding import PartitionSpec as P

C = 768
NB = 8
BS = 96
W = 360
KW = 176
H = 128
KH = 16
ENS = 8

ROWS = 8
WB = 8
COLS = KW // WB // 2
UNITS = COLS * KH
GC = C // 2
GB = NB // 2
AXES = ("dp", "row")

norm_eps = 1e-06
gelu_coef = 0.7978845608
cube_coef = 0.044715
bf16 = jnp.bfloat16
f32 = jnp.float32
COST = 0
VMEM_LIMIT = 48 * 1024 * 1024
VMEM_MOST = 62 * 1024 * 1024


def first_wave(col, core):
    return WB * (2 * col + (core + col) % 2)


def long_tables():
    firsts = np.array([[first_wave(col, core) for col in range(COLS)] for core in range(2)])
    ids = firsts[:, :, None] + np.arange(WB)
    angle = ((ids[..., None] * np.arange(W)) % W).astype(np.float64) * (2.0 * math.pi / W)
    forward = np.stack([np.cos(angle), -np.sin(angle)], axis=2).astype(np.float32)
    forward = forward / np.float32(math.sqrt(W))
    factor = np.where(ids == 0, 1.0, 2.0).astype(np.float32)[:, :, None, :, None]
    forward, inverse = (
        table.reshape(2, COLS * 2 * WB, W).astype(ml_dtypes.bfloat16)
        for table in (forward, forward * factor)
    )
    return forward, inverse


def latitude_table():
    modes = np.arange(KH)
    signed = np.where(modes < KH // 2, modes, modes - KH)
    angle = ((signed[:, None] * np.arange(H)) % H).astype(np.float64) * (2.0 * math.pi / H)
    cos = (np.cos(angle) / math.sqrt(H)).astype(np.float32).reshape(KH, H // ROWS, ROWS)
    sin = (np.sin(angle) / math.sqrt(H)).astype(np.float32).reshape(KH, H // ROWS, ROWS)
    mixed = np.stack([np.stack([cos, sin], -1), np.stack([-sin, cos], -1)], 1)
    whole = np.einsum("jprhq,kl->rjpkhql", mixed, np.eye(WB, dtype=np.float32))
    return whole.reshape(H // ROWS, KH * 2 * WB, ROWS * 2 * WB).astype(ml_dtypes.bfloat16)


def place(index):
    dp, row = divmod(index, 16)
    y, x_lo = divmod(dp, 2)
    z, rest = divmod(row, 4)
    x_hi, core = divmod(rest, 2)
    return x_hi * 2 + x_lo, y, z, core


def number(x, y, z, core):
    return (y * 2 + x % 2) * 16 + z * 4 + (x // 2) * 2 + core


def shift(array, dx, name):
    pairs = []
    for index in range(128):
        x, y, z, core = place(index)
        pairs.append((index, number((x + dx) % 4, y, z, core)))
    with jax.named_scope(name):
        return lax.ppermute(array, AXES, pairs)


def onward(array, name):
    pairs = []
    for index in range(128):
        x, y, z, core = place(index)
        pairs.append((index, number(x, y, (z + 1 + 2 * core) % 4, core)))
    with jax.named_scope(name):
        return lax.ppermute(array, AXES, pairs)


def swap(array, name, fx=0, fy=0, fz=0, fc=0):
    pairs = []
    for index in range(128):
        x, y, z, core = place(index)
        pairs.append((index, number(x ^ fx, y ^ fy, z ^ fz, core ^ fc)))
    with jax.named_scope(name):
        return lax.ppermute(array, AXES, pairs)


def call(kernel, name, grid, in_specs, out_specs, out_shape, scratch=(), flops=0, moved=0, limit=None):
    return pl.pallas_call(
        kernel,
        name=name,
        grid_spec=pltpu.PrefetchScalarGridSpec(
            num_scalar_prefetch=3,
            grid=grid,
            in_specs=in_specs,
            out_specs=out_specs,
            scratch_shapes=list(scratch),
        ),
        out_shape=out_shape,
        compiler_params=pltpu.CompilerParams(vmem_limit_bytes=limit or VMEM_LIMIT),
        cost_estimate=pl.CostEstimate(flops=COST*flops, bytes_accessed=COST*moved, transcendentals=0),
    )


def layer_norm(block):
    center = block.astype(f32)
    deviation = center - jnp.mean(center, axis=-1, keepdims=True)
    inverse_std = lax.rsqrt(jnp.mean(deviation * deviation, axis=-1, keepdims=True) + norm_eps)
    return deviation * inverse_std, inverse_std


def dot(left, right):
    return jnp.dot(left, right, preferred_element_type=f32)


def dot_nt(left, right):
    return lax.dot_general(left, right, (((1,), (1,)), ((), ())), preferred_element_type=f32)


def dot_tn(left, right):
    return lax.dot_general(left, right, (((0,), (0,)), ((), ())), preferred_element_type=f32)


def own_table(shape):
    return pl.BlockSpec((1,) + shape, lambda i, info, slots, cuts: (info[2], 0, 0))


def beside_table(shape):
    return pl.BlockSpec((1,) + shape, lambda i, info, slots, cuts: (1 - info[2], 0, 0))


def row_block(*shape):
    zeros = (0,) * (len(shape) - 1)
    return pl.BlockSpec(shape, lambda i, info, slots, cuts: (i,) + zeros)


def fixed(*shape):
    zeros = (0,) * len(shape)
    return pl.BlockSpec(shape, lambda i, info, slots, cuts: zeros)


def lon_forward(scalars, array, table, gain=None):
    step = 4

    def kernel(info, slots, cuts, own_t, beside_t, x, *rest):
        for at in range(step):
            if gain is None:
                own, beside = rest
                rows = x[at]
            else:
                scale, own, beside = rest
                rows = (layer_norm(x[at])[0] * scale[...].reshape(1, C)).astype(bf16)
            own[at] = dot(own_t[0], rows).astype(bf16).reshape(COLS, 2 * WB, C)
            beside[at] = dot(beside_t[0], rows).astype(bf16).reshape(COLS, 2 * WB, C)

    specs = [own_table((KW, W)), beside_table((KW, W)), row_block(step, W, C)]
    operands = [table, table, array]
    if gain is not None:
        specs.append(fixed(C))
        operands.append(gain)
    shape = jax.ShapeDtypeStruct((ROWS, COLS, 2 * WB, C), bf16)
    return call(
        kernel,
        "lon_forward",
        (ROWS // step,),
        specs,
        [row_block(step, COLS, 2 * WB, C)] * 2,
        [shape, shape],
        limit=VMEM_MOST,
        flops=2 * ROWS * 2 * KW * W * C,
        moved=2 * ROWS * C * (W + 2 * KW),
    )(*scalars, *operands)


def lane_block(lanes, *shape):
    zeros = (0,) * len(shape)
    return pl.BlockSpec(shape + (lanes,), lambda i, info, slots, cuts: zeros + (i,))


def lat_tables(shape):
    return [
        pl.BlockSpec((1,) + shape, lambda i, info, slots, cuts: (info[3], 0, 0)),
        pl.BlockSpec((1,) + shape, lambda i, info, slots, cuts: (info[4], 0, 0)),
    ]


LANES = 256


def slot_base(info, step, half, owned):
    return (lax.rem(info[0] + step * info[7], 4) * 2 + lax.rem(info[1] + half, 2)) * owned


def lat_forward(scalars, own, beside, table, owned):
    def kernel(info, slots, cuts, own_t, beside_t, x_own, x_beside, *rest):
        outs, over, units = rest[:8], rest[8], rest[9]
        mix = jnp.concatenate([own_t[0], beside_t[0]], axis=1)
        for col in range(COLS):
            rows = jnp.concatenate(
                [x_own[:, col].reshape(-1, LANES), x_beside[:, col].reshape(-1, LANES)], axis=0
            )
            units[col * KH : (col + 1) * KH] = dot(mix, rows).astype(bf16).reshape(KH, 2 * WB, LANES)
        units[UNITS] = jnp.zeros((2 * WB, LANES), bf16)
        for step in range(4):
            for half in range(2):
                base = slot_base(info, step, half, owned)
                for at in range(owned):
                    outs[step * 2 + half][at] = units[slots[base + at]]

        @pl.when(slots[8 * owned] < UNITS)
        def _():
            for at in range(UNITS - 8 * owned):
                over[at] = units[slots[8 * owned + at]]

    shape = jax.ShapeDtypeStruct((owned, 2 * WB, C), bf16)
    return call(
        kernel,
        "lat_forward",
        (C // LANES,),
        lat_tables((KH * 2 * WB, ROWS * 2 * WB)) + [lane_block(LANES, ROWS, COLS, 2 * WB)] * 2,
        [lane_block(LANES, owned, 2 * WB)] * 8 + [lane_block(LANES, UNITS - 8 * owned, 2 * WB)],
        [shape] * 8 + [jax.ShapeDtypeStruct((UNITS - 8 * owned, 2 * WB, C), bf16)],
        [pltpu.VMEM((UNITS + 1, 2 * WB, LANES), bf16)],
        limit=VMEM_MOST,
        flops=2 * 256 * 256 * C * COLS,
        moved=2 * C * 16 * (UNITS + 8 * owned),
    )(*scalars, table, table, own, beside)


def lat_inverse(scalars, pieces, over, table, owned):
    def kernel(info, slots, cuts, own_t, beside_t, *rest):
        arrived, (over, own, beside, units) = rest[:8], rest[8:]
        units[...] = jnp.zeros(units.shape, bf16)
        for step in range(4):
            for half in range(2):
                base = slot_base(info, step, half, owned)
                for at in range(owned):
                    units[slots[base + at]] = arrived[step * 2 + half][at]

        @pl.when(slots[8 * owned] < UNITS)
        def _():
            for at in range(UNITS - 8 * owned):
                units[slots[8 * owned + at]] = over[at]

        mix = jnp.concatenate([own_t[0], beside_t[0]], axis=0)
        for col in range(COLS):
            rows = dot(mix, units[col * KH : (col + 1) * KH].reshape(-1, LANES)).astype(bf16)
            half = ROWS * 2 * WB
            own[:, col] = rows[:half].reshape(ROWS, 2 * WB, LANES)
            beside[:, col] = rows[half:].reshape(ROWS, 2 * WB, LANES)

    shape = jax.ShapeDtypeStruct((ROWS, COLS, 2 * WB, C), bf16)
    return call(
        kernel,
        "lat_inverse",
        (C // LANES,),
        lat_tables((ROWS * 2 * WB, KH * 2 * WB)) + [lane_block(LANES, owned, 2 * WB)] * 8
        + [lane_block(LANES, UNITS - 8 * owned, 2 * WB)],
        [lane_block(LANES, ROWS, COLS, 2 * WB)] * 2,
        [shape, shape],
        [pltpu.VMEM((UNITS + 1, 2 * WB, LANES), bf16)],
        flops=2 * 256 * 256 * C * COLS,
        moved=2 * C * 16 * (UNITS + 8 * owned),
    )(*scalars, table, table, *pieces, over)


def grid_rows(own_t, beside_t, x_own, x_beside, at):
    own = dot(own_t[0], x_own[at].reshape(KW, C))
    return own + dot(beside_t[0], x_beside[at].reshape(KW, C))


def lon_inverse_fields(scalars, own, beside, table, fields):
    step = 2

    def kernel(info, slots, cuts, own_t, beside_t, x_own, x_beside, x, out):
        for at in range(step):
            grid = grid_rows(own_t, beside_t, x_own, x_beside, at)
            out[at] = (x[at].astype(f32) + grid).astype(bf16)

    return call(
        kernel,
        "lon_inverse_fields",
        (ROWS // step,),
        [own_table((W, KW)), beside_table((W, KW))]
        + [row_block(step, COLS, 2 * WB, C)] * 2
        + [row_block(step, W, C)],
        row_block(step, W, C),
        jax.ShapeDtypeStruct((ROWS, W, C), bf16),
        flops=2 * ROWS * 2 * KW * W * C,
        moved=2 * ROWS * C * (2 * W + 2 * KW),
    )(*scalars, table, table, own, beside, fields)


def lon_inverse_grad(scalars, own, beside, table, fields, cotangent, gain):
    step = 2

    def kernel(info, slots, cuts, own_t, beside_t, x_own, x_beside, x, cot, scale, out):
        for at in range(step):
            grid = grid_rows(own_t, beside_t, x_own, x_beside, at)
            normal, inverse_std = layer_norm(x[at])
            scaled = grid * scale[...].reshape(1, C)
            first = jnp.mean(scaled, axis=-1, keepdims=True)
            second = jnp.mean(scaled * normal, axis=-1, keepdims=True)
            grad = inverse_std * (scaled - first - normal * second)
            out[at] = (cot[at].astype(f32) + grad).astype(bf16)

    return call(
        kernel,
        "lon_inverse_grad",
        (ROWS // step,),
        [own_table((W, KW)), beside_table((W, KW))]
        + [row_block(step, COLS, 2 * WB, C)] * 2
        + [row_block(step, W, C)] * 2
        + [fixed(C)],
        row_block(step, W, C),
        jax.ShapeDtypeStruct((ROWS, W, C), bf16),
        limit=VMEM_MOST,
        flops=2 * ROWS * 2 * KW * W * C,
        moved=2 * ROWS * C * (3 * W + 2 * KW),
    )(*scalars, table, table, own, beside, fields, cotangent, gain)


def wide_weights(scalars, weights):
    def kernel(info, slots, cuts, w, out):
        row = lax.broadcasted_iota(jnp.int32, (BS, GC), 0)
        lane = lax.broadcasted_iota(jnp.int32, (BS, GC), 1)
        for layer in range(2):
            for block in range(GB):
                move = (lane == row + block * BS).astype(f32).astype(bf16)
                real = dot(w[layer, 0, block], move)
                imag = dot(w[layer, 1, block], move)
                top = slice(block * BS, (block + 1) * BS)
                low = slice(GC + block * BS, GC + (block + 1) * BS)
                out[layer, 0, top, :GC] = real.astype(bf16)
                out[layer, 0, top, GC:] = imag.astype(bf16)
                out[layer, 0, low, :GC] = (-imag).astype(bf16)
                out[layer, 0, low, GC:] = real.astype(bf16)

    return call(
        kernel,
        "wide_weights",
        (2,),
        [pl.BlockSpec((2, 2, GB, BS, BS), lambda i, info, slots, cuts: (0, 0, i, 0, 0))],
        pl.BlockSpec((2, 1, C, C), lambda i, info, slots, cuts: (0, i, 0, 0)),
        jax.ShapeDtypeStruct((2, 2, C, C), bf16),
        moved=2 * 5 * C * C,
    )(*scalars, weights)


def gelu_pair(values):
    inner = jnp.tanh(gelu_coef * (values + cube_coef * values * values * values))
    value = 0.5 * values * (1.0 + inner)
    slope = 0.5 * (1.0 + inner) + 0.5 * values * (1.0 - inner * inner) * gelu_coef * (
        1.0 + 3.0 * cube_coef * values * values
    )
    return (value, slope)


def own_first(info, owned):
    return (info[0] * 2 + info[5]) * owned


def kept_of(info, slots, cuts, place):
    unit = slots[place]
    col = lax.div(unit, KH)
    first = WB * (2 * col + lax.rem(info[2] + col, 2))
    return jnp.where(unit < UNITS, cuts[lax.rem(unit, KH)] - first, 0)


def each(count, step):
    if count > 24:
        pl.loop(0, count)(step)
    else:
        for at in range(count):
            step(at)


def unit_rows(at):
    return pl.ds(pl.multiple_of(at * WB, WB) if not isinstance(at, int) else at * WB, WB)


def gather_units(info, slots, cuts, left, right, held, first):
    row = lax.broadcasted_iota(jnp.int32, (WB, GC), 0)

    def step(at):
        unit = left[at].astype(f32)
        if right is not None:
            unit = unit + right[at].astype(f32)
        kept = row < kept_of(info, slots, cuts, first + at)
        held[unit_rows(at), :GC] = jnp.where(kept, unit[:WB], 0.0)
        held[unit_rows(at), GC:] = jnp.where(kept, unit[WB:], 0.0)

    each(left.shape[0], step)
    return held[...].astype(bf16)


def scatter_units(info, slots, cuts, held, out, first):
    row = lax.broadcasted_iota(jnp.int32, (WB, GC), 0)

    def step(at):
        kept = row < kept_of(info, slots, cuts, first + at)
        real = jnp.where(kept, held[unit_rows(at), :GC], 0.0)
        imag = jnp.where(kept, held[unit_rows(at), GC:], 0.0)
        out[at] = jnp.concatenate([real, imag], axis=0).astype(bf16)

    each(out.shape[0], step)


def group_block(rows):
    return pl.BlockSpec((1, rows, C), lambda i, info, slots, cuts: (i, 0, 0))


def weight_block(layer):
    return pl.BlockSpec((1, 1, C, C), lambda i, info, slots, cuts: (layer, i, 0, 0))


def spectral_forward(scalars, units, wide, biases, first=None):
    owned = units[0].shape[0]
    count = owned * WB

    def kernel(info, slots, cuts, xl, *rest):
        xr = rest[0] if len(units) == 2 else None
        w0, w1, bias, out, given, hidden, slope, held = rest[-8:]
        place = own_first(info, owned) if first is None else first
        given[0] = gather_units(info, slots, cuts, xl, xr, held, place)
        b0 = jnp.concatenate([bias[0, 0:1, :], bias[0, 1:2, :]], axis=1)
        b1 = jnp.concatenate([bias[1, 0:1, :], bias[1, 1:2, :]], axis=1)
        act, slope[0] = gelu_pair(dot(given[0], w0[0, 0]) + b0)
        hidden[0] = act.astype(bf16)
        held[...] = dot(hidden[0], w1[0, 0]) + b1
        scatter_units(info, slots, cuts, held, out, place)

    return call(
        kernel,
        "spectral_forward",
        (2,),
        [lane_block(GC, owned, 2 * WB)] * len(units)
        + [weight_block(0), weight_block(1), lane_block(GC, 2, 2)],
        [lane_block(GC, owned, 2 * WB)] + [group_block(count)] * 3,
        [jax.ShapeDtypeStruct((owned, 2 * WB, C), bf16)]
        + [jax.ShapeDtypeStruct((2, count, C), kind) for kind in (bf16, bf16, f32)],
        [pltpu.VMEM((count, C), f32)],
        flops=8 * count * C * C,
        moved=8 * C * C + 20 * count * C,
    )(*scalars, *units, wide, wide, biases)


def spectral_backward(scalars, units, wide, given, slope, first=None):
    owned = units[0].shape[0]
    count = owned * WB

    def kernel(info, slots, cuts, xl, *rest):
        xr = rest[0] if len(units) == 2 else None
        w0, w1, given, slope, out, upper, lower, sums, held = rest[-9:]
        place = own_first(info, owned) if first is None else first
        upper[0] = gather_units(info, slots, cuts, xl, xr, held, place)
        sums[0] = jnp.zeros(sums.shape[1:], f32)
        sums[0, 0:1, :] = jnp.sum(upper[0].astype(f32), axis=0, keepdims=True)
        low = (dot_nt(upper[0], w1[0, 0]) * slope[0]).astype(bf16)
        lower[0] = low
        sums[0, 1:2, :] = jnp.sum(low.astype(f32), axis=0, keepdims=True)
        held[...] = dot_nt(low, w0[0, 0])
        scatter_units(info, slots, cuts, held, out, place)
        sums[0, 2:3, :] = jnp.sum(held[...] * given[0].astype(f32), axis=0, keepdims=True)

    return call(
        kernel,
        "spectral_backward",
        (2,),
        [lane_block(GC, owned, 2 * WB)] * len(units)
        + [weight_block(0), weight_block(1), group_block(count), group_block(count)],
        [lane_block(GC, owned, 2 * WB)] + [group_block(count)] * 2 + [group_block(8)],
        [jax.ShapeDtypeStruct((owned, 2 * WB, C), bf16)]
        + [jax.ShapeDtypeStruct((2, count, C), bf16)] * 2
        + [jax.ShapeDtypeStruct((2, 8, C), f32)],
        [pltpu.VMEM((count, C), f32)],
        flops=8 * count * C * C,
        moved=8 * C * C + 20 * count * C,
    )(*scalars, *units, wide, wide, given, slope)


SHARE = 416
PIECE = SHARE // 4


def weight_sums(scalars, given, lower, hidden, upper, sums, more=None):
    count = given.shape[1]

    def group(rows, lanes=C):
        return pl.BlockSpec(
            (1, rows, lanes), lambda i, info, slots, cuts: (lax.rem(i + 1 + info[2], 2), 0, 0)
        )

    def kernel(info, slots, cuts, u0, y0, u1, y1, small, *rest):
        send, keep, out = rest[-3:]
        lane = lax.div(lax.broadcasted_iota(jnp.int32, (BS, GC), 1), BS)
        for layer, (u, y) in enumerate(((u0, y0), (u1, y1))):
            whole = dot_tn(u[0], y[0])
            real = whole[:GC, :GC] + whole[GC:, GC:]
            imag = whole[:GC, GC:] - whole[GC:, :GC]
            for part, value in enumerate((real, imag)):
                folded = value[:BS]
                for block in range(1, GB):
                    folded = jnp.where(lane == block, value[block * BS : (block + 1) * BS], folded)
                first = (layer * 2 + part) * BS
                out[first : first + BS, :] = folded
        out[4 * BS : 4 * BS + 8, :] = small[0, :, :GC]
        out[4 * BS + 8 : 4 * BS + 16, :] = small[0, :, GC:]
        out[4 * BS + 16 :, :] = jnp.zeros((SHARE - 4 * BS - 16, GC), f32)
        total = out[...]
        if more is not None:
            total = total + rest[0][0]

        @pl.when(pl.program_id(0) == 0)
        def _():
            send[...] = total.astype(send.dtype)

        @pl.when(pl.program_id(0) == 1)
        def _():
            keep[...] = total

    return call(
        kernel,
        "weight_sums",
        (2,),
        [group(count)] * 4 + [group(8)] + ([] if more is None else [group(SHARE, GC)]),
        [fixed(SHARE, GC)] * 2,
        [
            jax.ShapeDtypeStruct((SHARE, GC), f32 if more is None else bf16),
            jax.ShapeDtypeStruct((SHARE, GC), f32),
        ],
        [pltpu.VMEM((SHARE, GC), f32)],
    )(*scalars, given, lower, hidden, upper, sums, *([] if more is None else [more]))


def split_sum(scalars, left, right):
    def kernel(info, slots, cuts, left, right, *outs):
        for far in range(4):
            rows = pl.ds(pl.multiple_of(jnp.bitwise_xor(info[6], far) * PIECE, 8), PIECE)
            outs[far][...] = (left[rows, :] + right[rows, :].astype(f32)).astype(bf16)

    return call(
        kernel,
        "split_sum",
        (1,),
        [fixed(SHARE, GC)] * 2,
        [fixed(PIECE, GC)] * 4,
        [jax.ShapeDtypeStruct((PIECE, GC), bf16)] * 4,
        moved=16 * SHARE * GC,
    )(*scalars, left, right)


def place_sums(scalars, pieces, gain):
    spectral_scale = 1.0 / math.sqrt(ENS * KH * KW)
    gain_scale = 1.0 / math.sqrt(ENS * H * W)

    def kernel(info, slots, cuts, p0, p1, p2, p3, scale, weight_out, bias_out, gain_out, held):
        for far, piece in enumerate((p0, p1, p2, p3)):
            rows = pl.ds(pl.multiple_of(jnp.bitwise_xor(info[6], far) * PIECE, 8), PIECE)
            held[info[2], rows, :] = piece[0].astype(f32)
            held[1 - info[2], rows, :] = piece[1].astype(f32)
        for group in range(2):
            lanes = slice(group * GC, (group + 1) * GC)
            for layer in range(2):
                for part in range(2):
                    first = (layer * 2 + part) * BS
                    value = held[group, first : first + BS, :] * spectral_scale
                    for block in range(GB):
                        weight_out[layer, part, group * GB + block] = value[
                            :, block * BS : (block + 1) * BS
                        ]
                    at = 4 * BS + part * 8 + 1 - layer
                    bias_out[layer, part : part + 1, lanes] = (
                        held[group, at : at + 1, :] * spectral_scale
                    )
            at = 4 * BS + 2
            both = held[group, at : at + 1, :] + held[group, at + 8 : at + 9, :]
            gain_out[lanes] = (both * gain_scale).reshape(GC) / scale[lanes]

    return call(
        kernel,
        "place_sums",
        (1,),
        [fixed(2, PIECE, GC)] * 4 + [fixed(C)],
        [fixed(2, 2, NB, BS, BS), fixed(2, 2, C), fixed(C)],
        [
            jax.ShapeDtypeStruct((2, 2, NB, BS, BS), f32),
            jax.ShapeDtypeStruct((2, 2, C), f32),
            jax.ShapeDtypeStruct((C,), f32),
        ],
        [pltpu.VMEM((2, SHARE, GC), f32)],
        moved=16 * SHARE * GC,
    )(*scalars, *pieces, gain)


def add(*arrays):
    total = arrays[0].astype(f32)
    for array in arrays[1:]:
        total = total + array.astype(f32)
    return total.astype(bf16)


def four(own, first, second, third):
    own, first, second, third = (array.astype(f32) for array in (own, first, second, third))
    return ((own + first) + (second + third)).astype(bf16)


class Order:
    def __init__(self, info, slots, cutoffs):
        self.info, self.rest = info, (slots, cutoffs)

    @property
    def scalars(self):
        return (self.info,) + self.rest

    def ready(self, *arrays):
        return lax.optimization_barrier(arrays + (self.info,))[:-1]

    def wait(self, *arrays):
        *arrays, self.info = lax.optimization_barrier(tuple(arrays) + (self.info,))
        return arrays[0] if len(arrays) == 1 else arrays


def kept_units(cutoffs, core):
    col = jnp.arange(COLS, dtype=jnp.int32)[:, None]
    return (cutoffs[None, :] > first_wave(col, core)).astype(jnp.int32)


def unit_slots(cutoffs, core, total):
    unit = jnp.arange(UNITS, dtype=jnp.int32)[:, None, None]
    col = jnp.arange(COLS, dtype=jnp.int32)[None, :, None]
    mode = jnp.arange(KH, dtype=jnp.int32)[None, None, :]
    kept = kept_units(cutoffs, core)[None]
    rank = jnp.sum(jnp.where(col * KH + mode <= unit, kept, 0), axis=(1, 2))
    place_of = jnp.arange(total, dtype=jnp.int32)
    return jnp.sum((rank[None, :] <= place_of[:, None]).astype(jnp.int32), axis=1)


def past_slots(order, owned, f_over, g_over, wide, biases):
    groups = [[2 * at + core for at in range(8)] for core in range(2)]
    f_sum, g_sum = lax.psum(
        (f_over.astype(f32), g_over.astype(f32)), "row", axis_index_groups=groups
    )
    first = 8 * owned
    shrunk, given, hidden, slope = spectral_forward(
        order.scalars, (f_sum,), wide, biases, first
    )
    bottom, upper, lower, sums = spectral_backward(
        order.scalars, (g_sum,), wide, given, slope, first
    )
    other, own = weight_sums(order.scalars, given, lower, hidden, upper, sums)
    counted = (order.info[0] == 0) & (order.info[1] == 0)
    more = jnp.where(order.info[2] == 0, jnp.stack([own, other]), jnp.stack([other, own]))
    return shrunk, bottom, jnp.where(counted, more, 0.0)


def whole_pass(owned, field_in, grad_out, gain, weights, biases, cutoffs):
    dp = lax.axis_index("dp").astype(jnp.int32)
    row = lax.axis_index("row").astype(jnp.int32)
    z, x_hi, core = row // 4, (row // 2) % 2, row % 2
    y, x_lo = dp // 2, dp % 2
    half_owned = ((x_hi * 2 + x_lo + 3) % 4) // 2
    info = jnp.stack([z, x_hi, core, row, row + 1 - 2 * core, half_owned, y, 1 + 2 * core])
    order = Order(info, unit_slots(cutoffs, core, UNITS), cutoffs)
    most = jnp.maximum(jnp.sum(kept_units(cutoffs, 0)), jnp.sum(kept_units(cutoffs, 1)))
    wait, ready = order.wait, order.ready
    fwd_table, inv_table = long_tables()
    fwd_turned = jnp.asarray(fwd_table.transpose(0, 2, 1))
    inv_turned = jnp.asarray(inv_table.transpose(0, 2, 1))
    fwd_table, inv_table = jnp.asarray(fwd_table), jnp.asarray(inv_table)
    lat_np = latitude_table()
    lat_table = jnp.asarray(lat_np)
    lat_turned = jnp.asarray(lat_np.transpose(0, 2, 1))

    f_own, f_send = wait(*lon_forward(order.scalars, field_in, fwd_table, gain))
    f_recv = swap(f_send, "f_pair", fc=1)
    g_own, g_send = wait(*lon_forward(order.scalars, grad_out, inv_table))
    f_recv = wait(f_recv)
    g_recv = swap(*ready(g_send), "g_pair", fc=1)

    f0a, f0b, f1a, f1b, f2a, f2b, f3a, f3b, f_over = wait(
        *lat_forward(order.scalars, f_own, f_recv, lat_table, owned)
    )
    fa, fb = onward(f3a, "f3a"), onward(f3b, "f3b")
    g_recv = wait(g_recv)
    g0a, g0b, g1a, g1b, g2a, g2b, g3a, g3b, g_over = wait(
        *lat_forward(order.scalars, g_own, g_recv, lat_table, owned)
    )
    fa = onward(wait(add(f2a, wait(fa))), "f2a")
    fb = onward(wait(add(f2b, wait(fb))), "f2b")
    wide = wait(wide_weights(order.scalars, weights))
    fa = onward(wait(add(f1a, wait(fa))), "f1a")
    fb = onward(wait(add(f1b, wait(fb))), "f1b")
    left = shift(wait(add(f0a, wait(fa))), 1, "f_left")
    (ga,) = ready(g3a)
    ga = onward(ga, "g3a")
    right = shift(wait(add(f0b, wait(fb))), -1, "f_right")
    (gb,) = ready(g3b)
    gb = onward(gb, "g3b")
    ga = onward(wait(add(g2a, wait(ga))), "g2a")
    left = wait(left)
    right = wait(right)
    gb = onward(wait(add(g2b, wait(gb))), "g2b")

    shrunk, given, hidden, slope = wait(
        *spectral_forward(order.scalars, (left, right), wide, biases)
    )
    f0a, f0b = shift(shrunk, -1, "f_back_a"), shift(shrunk, 1, "f_back_b")
    ga = onward(wait(add(g1a, wait(ga))), "g1a")
    gb = onward(wait(add(g1b, wait(gb))), "g1b")
    f0a = wait(f0a)
    f3a = onward(f0a, "f_from3a")
    f0b = wait(f0b)
    f3b = onward(f0b, "f_from3b")
    left = shift(wait(add(g0a, wait(ga))), 1, "g_left")
    right = shift(wait(add(g0b, wait(gb))), -1, "g_right")
    start = ready(f_over, g_over, jnp.zeros((2, SHARE, GC), f32))
    _, f_over, g_over, more = lax.while_loop(
        lambda held: held[0] > 8 * owned,
        lambda held: (
            jnp.zeros((), jnp.int32),
            *past_slots(order, owned, held[1], held[2], wide, biases),
        ),
        (most, *start),
    )
    f_over, g_over, more = wait(f_over, g_over, more)
    f3a = wait(f3a)
    f2a = onward(f3a, "f_from2a")
    left = wait(left)
    right = wait(right)
    f3b = wait(f3b)
    f2b = onward(f3b, "f_from2b")

    bottom, upper, lower, sums = wait(
        *spectral_backward(order.scalars, (left, right), wide, given, slope)
    )
    g0a, g0b = shift(bottom, -1, "g_back_a"), shift(bottom, 1, "g_back_b")
    f2a = wait(f2a)
    f1a = onward(f2a, "f_from1a")
    f2b = wait(f2b)
    f1b = onward(f2b, "f_from1b")
    send, keep = wait(*weight_sums(order.scalars, given, lower, hidden, upper, sums, more))
    f1a = wait(f1a)
    g0a = wait(g0a)
    g3a = onward(g0a, "g_from3a")
    g0b = wait(g0b)
    g3b = onward(g0b, "g_from3b")
    f1b = wait(f1b)

    arrived = swap(*ready(send), "sum_core", fc=1)
    f_own, f_send = wait(
        *lat_inverse(
            order.scalars, (f0a, f0b, f1a, f1b, f2a, f2b, f3a, f3b), f_over, lat_turned, owned
        )
    )
    f_recv = swap(f_send, "f_pair_back", fc=1)
    g3a = wait(g3a)
    g2a = onward(g3a, "g_from2a")
    g3b = wait(g3b)
    g2b = onward(g3b, "g_from2b")
    arrived = wait(arrived)
    pieces = wait(*split_sum(order.scalars, keep, arrived))
    arrived = [
        swap(piece, "sum_y", fy=far) for far, piece in zip((1, 2, 3), ready(*pieces[1:]))
    ]
    g2a = wait(g2a)
    g1a = onward(g2a, "g_from1a")
    g2b = wait(g2b)
    g1b = onward(g2b, "g_from1b")
    arrived = wait(*arrived)
    total = wait(four(pieces[0], *arrived))
    beside = swap(total, "sum_x1", fx=1)
    g1a = wait(g1a)
    total = wait(add(total, wait(beside)))
    beside = swap(total, "sum_x2", fx=2)
    g1b = wait(g1b)
    total = wait(add(total, wait(beside)))
    beside = swap(total, "sum_z1", fz=1)
    g_own, g_send = wait(
        *lat_inverse(
            order.scalars, (g0a, g0b, g1a, g1b, g2a, g2b, g3a, g3b), g_over, lat_turned, owned
        )
    )
    g_recv = swap(g_send, "g_pair_back", fc=1)
    total = wait(add(total, wait(beside)))
    beside = swap(total, "sum_z2", fz=2)
    f_recv = wait(f_recv)
    block_out = wait(
        lon_inverse_fields(order.scalars, f_own, f_recv, inv_turned, field_in)
    )
    total = wait(add(total, wait(beside)))
    total = wait(jnp.stack([total, wait(swap(total, "all_core", fc=1))]))
    arrived = [swap(total, "all_y", fy=far) for far in (1, 2, 3)]
    g_recv = wait(g_recv)
    input_grad = wait(
        lon_inverse_grad(order.scalars, g_own, g_recv, fwd_turned, field_in, grad_out, gain)
    )
    arrived = wait(*arrived)
    weight_grads, bias_grads, gain_grad = place_sums(
        order.scalars, (total, *arrived), gain
    )
    return (block_out[None], input_grad[None], weight_grads, bias_grads, gain_grad)


def body(fields, cotangent, norm_gain, weights, biases, cutoffs):
    operands = (fields[0], cotangent[0], norm_gain, weights, biases, cutoffs)
    return whole_pass(OWNED, *operands)


OWNED = 16


def solution(mesh):
    placed = (P("dp", "row", None, None), P("dp", "row", None, None), P(), P(), P(), P())
    return jax.shard_map(
        body,
        mesh=mesh,
        in_specs=placed,
        out_specs=(P("dp", "row", None, None), P("dp", "row", None, None), P(), P(), P()),
        check_vma=False,
    )
```

```python
import functools
import math

import jax
import jax.numpy as jnp
import ml_dtypes
import numpy as np
from jax import lax
from jax.experimental import pallas as pl
from jax.experimental.pallas import tpu as pltpu
from jax.sharding import PartitionSpec as P

C = 768
NB = 8
BS = 96
W = 360
KW = 176
H = 128
KH = 16
ENS = 8

ROWS = 8
WB = 8
COLS = KW // WB // 2
UNITS = COLS * KH
GC = C // 2
GB = NB // 2
AXES = ("dp", "row")

norm_eps = 1e-06
gelu_coef = 0.7978845608
cube_coef = 0.044715
bf16 = jnp.bfloat16
f32 = jnp.float32
COST = 0
VMEM_LIMIT = 48 * 1024 * 1024
VMEM_MOST = 62 * 1024 * 1024


def first_wave(col, core):
    return WB * (2 * col + (core + col) % 2)


def long_tables():
    firsts = np.array([[first_wave(col, core) for col in range(COLS)] for core in range(2)])
    ids = firsts[:, :, None] + np.arange(WB)
    angle = ((ids[..., None] * np.arange(W)) % W).astype(np.float64) * (2.0 * math.pi / W)
    forward = np.stack([np.cos(angle), -np.sin(angle)], axis=2).astype(np.float32)
    forward = forward / np.float32(math.sqrt(W))
    factor = np.where(ids == 0, 1.0, 2.0).astype(np.float32)[:, :, None, :, None]
    forward, inverse = (
        table.reshape(2, COLS * 2 * WB, W).astype(ml_dtypes.bfloat16)
        for table in (forward, forward * factor)
    )
    return forward, inverse


def latitude_table():
    modes = np.arange(KH)
    signed = np.where(modes < KH // 2, modes, modes - KH)
    angle = ((signed[:, None] * np.arange(H)) % H).astype(np.float64) * (2.0 * math.pi / H)
    cos = (np.cos(angle) / math.sqrt(H)).astype(np.float32).reshape(KH, H // ROWS, ROWS)
    sin = (np.sin(angle) / math.sqrt(H)).astype(np.float32).reshape(KH, H // ROWS, ROWS)
    mixed = np.stack([np.stack([cos, sin], -1), np.stack([-sin, cos], -1)], 1)
    whole = np.einsum("jprhq,kl->rjpkhql", mixed, np.eye(WB, dtype=np.float32))
    return whole.reshape(H // ROWS, KH * 2 * WB, ROWS * 2 * WB).astype(ml_dtypes.bfloat16)


def place(index):
    dp, row = divmod(index, 16)
    y, x_lo = divmod(dp, 2)
    z, rest = divmod(row, 4)
    x_hi, core = divmod(rest, 2)
    return x_hi * 2 + x_lo, y, z, core


def number(x, y, z, core):
    return (y * 2 + x % 2) * 16 + z * 4 + (x // 2) * 2 + core


def shift(array, dx, name):
    pairs = []
    for index in range(128):
        x, y, z, core = place(index)
        pairs.append((index, number((x + dx) % 4, y, z, core)))
    with jax.named_scope(name):
        return lax.ppermute(array, AXES, pairs)


def onward(array, name):
    pairs = []
    for index in range(128):
        x, y, z, core = place(index)
        pairs.append((index, number(x, y, (z + 1 + 2 * core) % 4, core)))
    with jax.named_scope(name):
        return lax.ppermute(array, AXES, pairs)


def swap(array, name, fx=0, fy=0, fz=0, fc=0):
    pairs = []
    for index in range(128):
        x, y, z, core = place(index)
        pairs.append((index, number(x ^ fx, y ^ fy, z ^ fz, core ^ fc)))
    with jax.named_scope(name):
        return lax.ppermute(array, AXES, pairs)


def call(kernel, name, grid, in_specs, out_specs, out_shape, scratch=(), flops=0, moved=0, limit=None):
    return pl.pallas_call(
        kernel,
        name=name,
        grid_spec=pltpu.PrefetchScalarGridSpec(
            num_scalar_prefetch=3,
            grid=grid,
            in_specs=in_specs,
            out_specs=out_specs,
            scratch_shapes=list(scratch),
        ),
        out_shape=out_shape,
        compiler_params=pltpu.CompilerParams(vmem_limit_bytes=limit or VMEM_LIMIT),
        cost_estimate=pl.CostEstimate(flops=COST*flops, bytes_accessed=COST*moved, transcendentals=0),
    )


def layer_norm(block):
    center = block.astype(f32)
    deviation = center - jnp.mean(center, axis=-1, keepdims=True)
    inverse_std = lax.rsqrt(jnp.mean(deviation * deviation, axis=-1, keepdims=True) + norm_eps)
    return deviation * inverse_std, inverse_std


def dot(left, right):
    return jnp.dot(left, right, preferred_element_type=f32)


def dot_nt(left, right):
    return lax.dot_general(left, right, (((1,), (1,)), ((), ())), preferred_element_type=f32)


def dot_tn(left, right):
    return lax.dot_general(left, right, (((0,), (0,)), ((), ())), preferred_element_type=f32)


def own_table(shape):
    return pl.BlockSpec((1,) + shape, lambda i, info, slots, cuts: (info[2], 0, 0))


def beside_table(shape):
    return pl.BlockSpec((1,) + shape, lambda i, info, slots, cuts: (1 - info[2], 0, 0))


def row_block(*shape):
    zeros = (0,) * (len(shape) - 1)
    return pl.BlockSpec(shape, lambda i, info, slots, cuts: (i,) + zeros)


def fixed(*shape):
    zeros = (0,) * len(shape)
    return pl.BlockSpec(shape, lambda i, info, slots, cuts: zeros)


def lon_forward(scalars, array, table, gain=None):
    step = 4

    def kernel(info, slots, cuts, own_t, beside_t, x, *rest):
        for at in range(step):
            if gain is None:
                own, beside = rest
                rows = x[at]
            else:
                scale, own, beside = rest
                rows = (layer_norm(x[at])[0] * scale[...].reshape(1, C)).astype(bf16)
            own[at] = dot(own_t[0], rows).astype(bf16).reshape(COLS, 2 * WB, C)
            beside[at] = dot(beside_t[0], rows).astype(bf16).reshape(COLS, 2 * WB, C)

    specs = [own_table((KW, W)), beside_table((KW, W)), row_block(step, W, C)]
    operands = [table, table, array]
    if gain is not None:
        specs.append(fixed(C))
        operands.append(gain)
    shape = jax.ShapeDtypeStruct((ROWS, COLS, 2 * WB, C), bf16)
    return call(
        kernel,
        "lon_forward",
        (ROWS // step,),
        specs,
        [row_block(step, COLS, 2 * WB, C)] * 2,
        [shape, shape],
        limit=VMEM_MOST,
        flops=2 * ROWS * 2 * KW * W * C,
        moved=2 * ROWS * C * (W + 2 * KW),
    )(*scalars, *operands)


def lane_block(lanes, *shape):
    zeros = (0,) * len(shape)
    return pl.BlockSpec(shape + (lanes,), lambda i, info, slots, cuts: zeros + (i,))


def lat_tables(shape):
    return [
        pl.BlockSpec((1,) + shape, lambda i, info, slots, cuts: (info[3], 0, 0)),
        pl.BlockSpec((1,) + shape, lambda i, info, slots, cuts: (info[4], 0, 0)),
    ]


LANES = 384


def slot_base(info, step, half, owned):
    return (lax.rem(info[0] + step * info[7], 4) * 2 + lax.rem(info[1] + half, 2)) * owned


def lat_forward(scalars, own, beside, table, owned):
    def kernel(info, slots, cuts, own_t, beside_t, x_own, x_beside, *rest):
        outs, over, units = rest[:8], rest[8], rest[9]
        mix = jnp.concatenate([own_t[0], beside_t[0]], axis=1)
        for col in range(COLS):
            rows = jnp.concatenate(
                [x_own[:, col].reshape(-1, LANES), x_beside[:, col].reshape(-1, LANES)], axis=0
            )
            units[col * KH : (col + 1) * KH] = dot(mix, rows).astype(bf16).reshape(KH, 2 * WB, LANES)
        units[UNITS] = jnp.zeros((2 * WB, LANES), bf16)
        for step in range(4):
            for half in range(2):
                base = slot_base(info, step, half, owned)
                for at in range(owned):
                    outs[step * 2 + half][at] = units[slots[base + at]]

        @pl.when(slots[8 * owned] < UNITS)
        def _():
            for at in range(UNITS - 8 * owned):
                over[at] = units[slots[8 * owned + at]]

    shape = jax.ShapeDtypeStruct((owned, 2 * WB, C), bf16)
    return call(
        kernel,
        "lat_forward",
        (C // LANES,),
        lat_tables((KH * 2 * WB, ROWS * 2 * WB)) + [lane_block(LANES, ROWS, COLS, 2 * WB)] * 2,
        [lane_block(LANES, owned, 2 * WB)] * 8 + [lane_block(LANES, UNITS - 8 * owned, 2 * WB)],
        [shape] * 8 + [jax.ShapeDtypeStruct((UNITS - 8 * owned, 2 * WB, C), bf16)],
        [pltpu.VMEM((UNITS + 1, 2 * WB, LANES), bf16)],
        limit=VMEM_MOST,
        flops=2 * 256 * 256 * C * COLS,
        moved=2 * C * 16 * (UNITS + 8 * owned),
    )(*scalars, table, table, own, beside)


def lat_inverse(scalars, pieces, over, table, owned):
    def kernel(info, slots, cuts, own_t, beside_t, *rest):
        arrived, (over, own, beside, units) = rest[:8], rest[8:]
        units[...] = jnp.zeros(units.shape, bf16)
        for step in range(4):
            for half in range(2):
                base = slot_base(info, step, half, owned)
                for at in range(owned):
                    units[slots[base + at]] = arrived[step * 2 + half][at]

        @pl.when(slots[8 * owned] < UNITS)
        def _():
            for at in range(UNITS - 8 * owned):
                units[slots[8 * owned + at]] = over[at]

        mix = jnp.concatenate([own_t[0], beside_t[0]], axis=0)
        for col in range(COLS):
            rows = dot(mix, units[col * KH : (col + 1) * KH].reshape(-1, LANES)).astype(bf16)
            half = ROWS * 2 * WB
            own[:, col] = rows[:half].reshape(ROWS, 2 * WB, LANES)
            beside[:, col] = rows[half:].reshape(ROWS, 2 * WB, LANES)

    shape = jax.ShapeDtypeStruct((ROWS, COLS, 2 * WB, C), bf16)
    return call(
        kernel,
        "lat_inverse",
        (C // LANES,),
        lat_tables((ROWS * 2 * WB, KH * 2 * WB)) + [lane_block(LANES, owned, 2 * WB)] * 8
        + [lane_block(LANES, UNITS - 8 * owned, 2 * WB)],
        [lane_block(LANES, ROWS, COLS, 2 * WB)] * 2,
        [shape, shape],
        [pltpu.VMEM((UNITS + 1, 2 * WB, LANES), bf16)],
        flops=2 * 256 * 256 * C * COLS,
        moved=2 * C * 16 * (UNITS + 8 * owned),
    )(*scalars, table, table, *pieces, over)


def grid_rows(own_t, beside_t, x_own, x_beside, at):
    own = dot(own_t[0], x_own[at].reshape(KW, C))
    return own + dot(beside_t[0], x_beside[at].reshape(KW, C))


def lon_inverse_fields(scalars, own, beside, table, fields):
    step = 2

    def kernel(info, slots, cuts, own_t, beside_t, x_own, x_beside, x, out):
        for at in range(step):
            grid = grid_rows(own_t, beside_t, x_own, x_beside, at)
            out[at] = (x[at].astype(f32) + grid).astype(bf16)

    return call(
        kernel,
        "lon_inverse_fields",
        (ROWS // step,),
        [own_table((W, KW)), beside_table((W, KW))]
        + [row_block(step, COLS, 2 * WB, C)] * 2
        + [row_block(step, W, C)],
        row_block(step, W, C),
        jax.ShapeDtypeStruct((ROWS, W, C), bf16),
        flops=2 * ROWS * 2 * KW * W * C,
        moved=2 * ROWS * C * (2 * W + 2 * KW),
    )(*scalars, table, table, own, beside, fields)


def lon_inverse_grad(scalars, own, beside, table, fields, cotangent, gain):
    step = 2

    def kernel(info, slots, cuts, own_t, beside_t, x_own, x_beside, x, cot, scale, out):
        for at in range(step):
            grid = grid_rows(own_t, beside_t, x_own, x_beside, at)
            normal, inverse_std = layer_norm(x[at])
            scaled = grid * scale[...].reshape(1, C)
            first = jnp.mean(scaled, axis=-1, keepdims=True)
            second = jnp.mean(scaled * normal, axis=-1, keepdims=True)
            grad = inverse_std * (scaled - first - normal * second)
            out[at] = (cot[at].astype(f32) + grad).astype(bf16)

    return call(
        kernel,
        "lon_inverse_grad",
        (ROWS // step,),
        [own_table((W, KW)), beside_table((W, KW))]
        + [row_block(step, COLS, 2 * WB, C)] * 2
        + [row_block(step, W, C)] * 2
        + [fixed(C)],
        row_block(step, W, C),
        jax.ShapeDtypeStruct((ROWS, W, C), bf16),
        limit=VMEM_MOST,
        flops=2 * ROWS * 2 * KW * W * C,
        moved=2 * ROWS * C * (3 * W + 2 * KW),
    )(*scalars, table, table, own, beside, fields, cotangent, gain)


def wide_weights(scalars, weights):
    def kernel(info, slots, cuts, w, out):
        row = lax.broadcasted_iota(jnp.int32, (BS, GC), 0)
        lane = lax.broadcasted_iota(jnp.int32, (BS, GC), 1)
        for layer in range(2):
            for block in range(GB):
                move = (lane == row + block * BS).astype(f32).astype(bf16)
                real = dot(w[layer, 0, block], move)
                imag = dot(w[layer, 1, block], move)
                top = slice(block * BS, (block + 1) * BS)
                low = slice(GC + block * BS, GC + (block + 1) * BS)
                out[layer, 0, top, :GC] = real.astype(bf16)
                out[layer, 0, top, GC:] = imag.astype(bf16)
                out[layer, 0, low, :GC] = (-imag).astype(bf16)
                out[layer, 0, low, GC:] = real.astype(bf16)

    return call(
        kernel,
        "wide_weights",
        (2,),
        [pl.BlockSpec((2, 2, GB, BS, BS), lambda i, info, slots, cuts: (0, 0, i, 0, 0))],
        pl.BlockSpec((2, 1, C, C), lambda i, info, slots, cuts: (0, i, 0, 0)),
        jax.ShapeDtypeStruct((2, 2, C, C), bf16),
        moved=2 * 5 * C * C,
    )(*scalars, weights)


def gelu_pair(values):
    inner = jnp.tanh(gelu_coef * (values + cube_coef * values * values * values))
    value = 0.5 * values * (1.0 + inner)
    slope = 0.5 * (1.0 + inner) + 0.5 * values * (1.0 - inner * inner) * gelu_coef * (
        1.0 + 3.0 * cube_coef * values * values
    )
    return (value, slope)


def own_first(info, owned):
    return (info[0] * 2 + info[5]) * owned


def kept_of(info, slots, cuts, place):
    unit = slots[place]
    col = lax.div(unit, KH)
    first = WB * (2 * col + lax.rem(info[2] + col, 2))
    return jnp.where(unit < UNITS, cuts[lax.rem(unit, KH)] - first, 0)


def each(count, step):
    if count > 24:
        pl.loop(0, count)(step)
    else:
        for at in range(count):
            step(at)


def unit_rows(at):
    return pl.ds(pl.multiple_of(at * WB, WB) if not isinstance(at, int) else at * WB, WB)


def gather_units(info, slots, cuts, left, right, held, first):
    row = lax.broadcasted_iota(jnp.int32, (WB, GC), 0)

    def step(at):
        unit = left[at].astype(f32)
        if right is not None:
            unit = unit + right[at].astype(f32)
        kept = row < kept_of(info, slots, cuts, first + at)
        held[unit_rows(at), :GC] = jnp.where(kept, unit[:WB], 0.0)
        held[unit_rows(at), GC:] = jnp.where(kept, unit[WB:], 0.0)

    each(left.shape[0], step)
    return held[...].astype(bf16)


def scatter_units(info, slots, cuts, held, out, first):
    row = lax.broadcasted_iota(jnp.int32, (WB, GC), 0)

    def step(at):
        kept = row < kept_of(info, slots, cuts, first + at)
        real = jnp.where(kept, held[unit_rows(at), :GC], 0.0)
        imag = jnp.where(kept, held[unit_rows(at), GC:], 0.0)
        out[at] = jnp.concatenate([real, imag], axis=0).astype(bf16)

    each(out.shape[0], step)


def group_block(rows):
    return pl.BlockSpec((1, rows, C), lambda i, info, slots, cuts: (i, 0, 0))


def weight_block(layer):
    return pl.BlockSpec((1, 1, C, C), lambda i, info, slots, cuts: (layer, i, 0, 0))


def spectral_forward(scalars, units, wide, biases, first=None):
    owned = units[0].shape[0]
    count = owned * WB

    def kernel(info, slots, cuts, xl, *rest):
        xr = rest[0] if len(units) == 2 else None
        w0, w1, bias, out, given, hidden, slope, held = rest[-8:]
        place = own_first(info, owned) if first is None else first
        given[0] = gather_units(info, slots, cuts, xl, xr, held, place)
        b0 = jnp.concatenate([bias[0, 0:1, :], bias[0, 1:2, :]], axis=1)
        b1 = jnp.concatenate([bias[1, 0:1, :], bias[1, 1:2, :]], axis=1)
        act, slope[0] = gelu_pair(dot(given[0], w0[0, 0]) + b0)
        hidden[0] = act.astype(bf16)
        held[...] = dot(hidden[0], w1[0, 0]) + b1
        scatter_units(info, slots, cuts, held, out, place)

    return call(
        kernel,
        "spectral_forward",
        (2,),
        [lane_block(GC, owned, 2 * WB)] * len(units)
        + [weight_block(0), weight_block(1), lane_block(GC, 2, 2)],
        [lane_block(GC, owned, 2 * WB)] + [group_block(count)] * 3,
        [jax.ShapeDtypeStruct((owned, 2 * WB, C), bf16)]
        + [jax.ShapeDtypeStruct((2, count, C), kind) for kind in (bf16, bf16, f32)],
        [pltpu.VMEM((count, C), f32)],
        flops=8 * count * C * C,
        moved=8 * C * C + 20 * count * C,
    )(*scalars, *units, wide, wide, biases)


def spectral_backward(scalars, units, wide, given, slope, first=None):
    owned = units[0].shape[0]
    count = owned * WB

    def kernel(info, slots, cuts, xl, *rest):
        xr = rest[0] if len(units) == 2 else None
        w0, w1, given, slope, out, upper, lower, sums, held = rest[-9:]
        place = own_first(info, owned) if first is None else first
        upper[0] = gather_units(info, slots, cuts, xl, xr, held, place)
        sums[0] = jnp.zeros(sums.shape[1:], f32)
        sums[0, 0:1, :] = jnp.sum(upper[0].astype(f32), axis=0, keepdims=True)
        low = (dot_nt(upper[0], w1[0, 0]) * slope[0]).astype(bf16)
        lower[0] = low
        sums[0, 1:2, :] = jnp.sum(low.astype(f32), axis=0, keepdims=True)
        held[...] = dot_nt(low, w0[0, 0])
        scatter_units(info, slots, cuts, held, out, place)
        sums[0, 2:3, :] = jnp.sum(held[...] * given[0].astype(f32), axis=0, keepdims=True)

    return call(
        kernel,
        "spectral_backward",
        (2,),
        [lane_block(GC, owned, 2 * WB)] * len(units)
        + [weight_block(0), weight_block(1), group_block(count), group_block(count)],
        [lane_block(GC, owned, 2 * WB)] + [group_block(count)] * 2 + [group_block(8)],
        [jax.ShapeDtypeStruct((owned, 2 * WB, C), bf16)]
        + [jax.ShapeDtypeStruct((2, count, C), bf16)] * 2
        + [jax.ShapeDtypeStruct((2, 8, C), f32)],
        [pltpu.VMEM((count, C), f32)],
        flops=8 * count * C * C,
        moved=8 * C * C + 20 * count * C,
    )(*scalars, *units, wide, wide, given, slope)


SHARE = 416
PIECE = SHARE // 4


def weight_sums(scalars, given, lower, hidden, upper, sums, more=None):
    count = given.shape[1]

    def group(rows, lanes=C):
        return pl.BlockSpec(
            (1, rows, lanes), lambda i, info, slots, cuts: (lax.rem(i + 1 + info[2], 2), 0, 0)
        )

    def kernel(info, slots, cuts, u0, y0, u1, y1, small, *rest):
        send, keep, out = rest[-3:]
        lane = lax.div(lax.broadcasted_iota(jnp.int32, (BS, GC), 1), BS)
        for layer, (u, y) in enumerate(((u0, y0), (u1, y1))):
            whole = dot_tn(u[0], y[0])
            real = whole[:GC, :GC] + whole[GC:, GC:]
            imag = whole[:GC, GC:] - whole[GC:, :GC]
            for part, value in enumerate((real, imag)):
                folded = value[:BS]
                for block in range(1, GB):
                    folded = jnp.where(lane == block, value[block * BS : (block + 1) * BS], folded)
                first = (layer * 2 + part) * BS
                out[first : first + BS, :] = folded
        out[4 * BS : 4 * BS + 8, :] = small[0, :, :GC]
        out[4 * BS + 8 : 4 * BS + 16, :] = small[0, :, GC:]
        out[4 * BS + 16 :, :] = jnp.zeros((SHARE - 4 * BS - 16, GC), f32)
        total = out[...]
        if more is not None:
            total = total + rest[0][0]

        @pl.when(pl.program_id(0) == 0)
        def _():
            send[...] = total.astype(send.dtype)

        @pl.when(pl.program_id(0) == 1)
        def _():
            keep[...] = total

    return call(
        kernel,
        "weight_sums",
        (2,),
        [group(count)] * 4 + [group(8)] + ([] if more is None else [group(SHARE, GC)]),
        [fixed(SHARE, GC)] * 2,
        [
            jax.ShapeDtypeStruct((SHARE, GC), f32 if more is None else bf16),
            jax.ShapeDtypeStruct((SHARE, GC), f32),
        ],
        [pltpu.VMEM((SHARE, GC), f32)],
    )(*scalars, given, lower, hidden, upper, sums, *([] if more is None else [more]))


def split_sum(scalars, left, right):
    def kernel(info, slots, cuts, left, right, *outs):
        for far in range(4):
            rows = pl.ds(pl.multiple_of(jnp.bitwise_xor(info[6], far) * PIECE, 8), PIECE)
            outs[far][...] = (left[rows, :] + right[rows, :].astype(f32)).astype(bf16)

    return call(
        kernel,
        "split_sum",
        (1,),
        [fixed(SHARE, GC)] * 2,
        [fixed(PIECE, GC)] * 4,
        [jax.ShapeDtypeStruct((PIECE, GC), bf16)] * 4,
        moved=16 * SHARE * GC,
    )(*scalars, left, right)


def place_sums(scalars, pieces, gain):
    spectral_scale = 1.0 / math.sqrt(ENS * KH * KW)
    gain_scale = 1.0 / math.sqrt(ENS * H * W)

    def kernel(info, slots, cuts, p0, p1, p2, p3, scale, weight_out, bias_out, gain_out, held):
        for far, piece in enumerate((p0, p1, p2, p3)):
            rows = pl.ds(pl.multiple_of(jnp.bitwise_xor(info[6], far) * PIECE, 8), PIECE)
            held[info[2], rows, :] = piece[0].astype(f32)
            held[1 - info[2], rows, :] = piece[1].astype(f32)
        for group in range(2):
            lanes = slice(group * GC, (group + 1) * GC)
            for layer in range(2):
                for part in range(2):
                    first = (layer * 2 + part) * BS
                    value = held[group, first : first + BS, :] * spectral_scale
                    for block in range(GB):
                        weight_out[layer, part, group * GB + block] = value[
                            :, block * BS : (block + 1) * BS
                        ]
                    at = 4 * BS + part * 8 + 1 - layer
                    bias_out[layer, part : part + 1, lanes] = (
                        held[group, at : at + 1, :] * spectral_scale
                    )
            at = 4 * BS + 2
            both = held[group, at : at + 1, :] + held[group, at + 8 : at + 9, :]
            gain_out[lanes] = (both * gain_scale).reshape(GC) / scale[lanes]

    return call(
        kernel,
        "place_sums",
        (1,),
        [fixed(2, PIECE, GC)] * 4 + [fixed(C)],
        [fixed(2, 2, NB, BS, BS), fixed(2, 2, C), fixed(C)],
        [
            jax.ShapeDtypeStruct((2, 2, NB, BS, BS), f32),
            jax.ShapeDtypeStruct((2, 2, C), f32),
            jax.ShapeDtypeStruct((C,), f32),
        ],
        [pltpu.VMEM((2, SHARE, GC), f32)],
        moved=16 * SHARE * GC,
    )(*scalars, *pieces, gain)


def add(*arrays):
    total = arrays[0].astype(f32)
    for array in arrays[1:]:
        total = total + array.astype(f32)
    return total.astype(bf16)


def four(own, first, second, third):
    own, first, second, third = (array.astype(f32) for array in (own, first, second, third))
    return ((own + first) + (second + third)).astype(bf16)


class Order:
    def __init__(self, info, slots, cutoffs):
        self.info, self.rest = info, (slots, cutoffs)

    @property
    def scalars(self):
        return (self.info,) + self.rest

    def ready(self, *arrays):
        return lax.optimization_barrier(arrays + (self.info,))[:-1]

    def wait(self, *arrays):
        *arrays, self.info = lax.optimization_barrier(tuple(arrays) + (self.info,))
        return arrays[0] if len(arrays) == 1 else arrays


def kept_units(cutoffs, core):
    col = jnp.arange(COLS, dtype=jnp.int32)[:, None]
    return (cutoffs[None, :] > first_wave(col, core)).astype(jnp.int32)


def unit_slots(cutoffs, core, total):
    unit = jnp.arange(UNITS, dtype=jnp.int32)[:, None, None]
    col = jnp.arange(COLS, dtype=jnp.int32)[None, :, None]
    mode = jnp.arange(KH, dtype=jnp.int32)[None, None, :]
    kept = kept_units(cutoffs, core)[None]
    rank = jnp.sum(jnp.where(col * KH + mode <= unit, kept, 0), axis=(1, 2))
    place_of = jnp.arange(total, dtype=jnp.int32)
    return jnp.sum((rank[None, :] <= place_of[:, None]).astype(jnp.int32), axis=1)


def past_slots(order, owned, f_over, g_over, wide, biases):
    groups = [[2 * at + core for at in range(8)] for core in range(2)]
    f_sum, g_sum = lax.psum(
        (f_over.astype(f32), g_over.astype(f32)), "row", axis_index_groups=groups
    )
    first = 8 * owned
    shrunk, given, hidden, slope = spectral_forward(
        order.scalars, (f_sum,), wide, biases, first
    )
    bottom, upper, lower, sums = spectral_backward(
        order.scalars, (g_sum,), wide, given, slope, first
    )
    other, own = weight_sums(order.scalars, given, lower, hidden, upper, sums)
    counted = (order.info[0] == 0) & (order.info[1] == 0)
    more = jnp.where(order.info[2] == 0, jnp.stack([own, other]), jnp.stack([other, own]))
    return shrunk, bottom, jnp.where(counted, more, 0.0)


def whole_pass(owned, field_in, grad_out, gain, weights, biases, cutoffs):
    dp = lax.axis_index("dp").astype(jnp.int32)
    row = lax.axis_index("row").astype(jnp.int32)
    z, x_hi, core = row // 4, (row // 2) % 2, row % 2
    y, x_lo = dp // 2, dp % 2
    half_owned = ((x_hi * 2 + x_lo + 3) % 4) // 2
    info = jnp.stack([z, x_hi, core, row, row + 1 - 2 * core, half_owned, y, 1 + 2 * core])
    order = Order(info, unit_slots(cutoffs, core, UNITS), cutoffs)
    most = jnp.maximum(jnp.sum(kept_units(cutoffs, 0)), jnp.sum(kept_units(cutoffs, 1)))
    wait, ready = order.wait, order.ready
    fwd_table, inv_table = long_tables()
    fwd_turned = jnp.asarray(fwd_table.transpose(0, 2, 1))
    inv_turned = jnp.asarray(inv_table.transpose(0, 2, 1))
    fwd_table, inv_table = jnp.asarray(fwd_table), jnp.asarray(inv_table)
    lat_np = latitude_table()
    lat_table = jnp.asarray(lat_np)
    lat_turned = jnp.asarray(lat_np.transpose(0, 2, 1))

    f_own, f_send = wait(*lon_forward(order.scalars, field_in, fwd_table, gain))
    f_recv = swap(f_send, "f_pair", fc=1)
    g_own, g_send = wait(*lon_forward(order.scalars, grad_out, inv_table))
    f_recv = wait(f_recv)
    g_recv = swap(*ready(g_send), "g_pair", fc=1)

    f0a, f0b, f1a, f1b, f2a, f2b, f3a, f3b, f_over = wait(
        *lat_forward(order.scalars, f_own, f_recv, lat_table, owned)
    )
    fa, fb = onward(f3a, "f3a"), onward(f3b, "f3b")
    g_recv = wait(g_recv)
    g0a, g0b, g1a, g1b, g2a, g2b, g3a, g3b, g_over = wait(
        *lat_forward(order.scalars, g_own, g_recv, lat_table, owned)
    )
    fa = onward(wait(add(f2a, wait(fa))), "f2a")
    fb = onward(wait(add(f2b, wait(fb))), "f2b")
    wide = wait(wide_weights(order.scalars, weights))
    fa = onward(wait(add(f1a, wait(fa))), "f1a")
    fb = onward(wait(add(f1b, wait(fb))), "f1b")
    left = shift(wait(add(f0a, wait(fa))), 1, "f_left")
    (ga,) = ready(g3a)
    ga = onward(ga, "g3a")
    right = shift(wait(add(f0b, wait(fb))), -1, "f_right")
    (gb,) = ready(g3b)
    gb = onward(gb, "g3b")
    ga = onward(wait(add(g2a, wait(ga))), "g2a")
    left = wait(left)
    right = wait(right)
    gb = onward(wait(add(g2b, wait(gb))), "g2b")

    shrunk, given, hidden, slope = wait(
        *spectral_forward(order.scalars, (left, right), wide, biases)
    )
    f0a, f0b = shift(shrunk, -1, "f_back_a"), shift(shrunk, 1, "f_back_b")
    ga = onward(wait(add(g1a, wait(ga))), "g1a")
    gb = onward(wait(add(g1b, wait(gb))), "g1b")
    f0a = wait(f0a)
    f3a = onward(f0a, "f_from3a")
    f0b = wait(f0b)
    f3b = onward(f0b, "f_from3b")
    left = shift(wait(add(g0a, wait(ga))), 1, "g_left")
    right = shift(wait(add(g0b, wait(gb))), -1, "g_right")
    start = ready(f_over, g_over, jnp.zeros((2, SHARE, GC), f32))
    _, f_over, g_over, more = lax.while_loop(
        lambda held: held[0] > 8 * owned,
        lambda held: (
            jnp.zeros((), jnp.int32),
            *past_slots(order, owned, held[1], held[2], wide, biases),
        ),
        (most, *start),
    )
    f_over, g_over, more = wait(f_over, g_over, more)
    f3a = wait(f3a)
    f2a = onward(f3a, "f_from2a")
    left = wait(left)
    right = wait(right)
    f3b = wait(f3b)
    f2b = onward(f3b, "f_from2b")

    bottom, upper, lower, sums = wait(
        *spectral_backward(order.scalars, (left, right), wide, given, slope)
    )
    g0a, g0b = shift(bottom, -1, "g_back_a"), shift(bottom, 1, "g_back_b")
    f2a = wait(f2a)
    f1a = onward(f2a, "f_from1a")
    f2b = wait(f2b)
    f1b = onward(f2b, "f_from1b")
    send, keep = wait(*weight_sums(order.scalars, given, lower, hidden, upper, sums, more))
    f1a = wait(f1a)
    g0a = wait(g0a)
    g3a = onward(g0a, "g_from3a")
    g0b = wait(g0b)
    g3b = onward(g0b, "g_from3b")
    f1b = wait(f1b)

    arrived = swap(*ready(send), "sum_core", fc=1)
    f_own, f_send = wait(
        *lat_inverse(
            order.scalars, (f0a, f0b, f1a, f1b, f2a, f2b, f3a, f3b), f_over, lat_turned, owned
        )
    )
    f_recv = swap(f_send, "f_pair_back", fc=1)
    g3a = wait(g3a)
    g2a = onward(g3a, "g_from2a")
    g3b = wait(g3b)
    g2b = onward(g3b, "g_from2b")
    arrived = wait(arrived)
    pieces = wait(*split_sum(order.scalars, keep, arrived))
    arrived = [
        swap(piece, "sum_y", fy=far) for far, piece in zip((1, 2, 3), ready(*pieces[1:]))
    ]
    g2a = wait(g2a)
    g1a = onward(g2a, "g_from1a")
    g2b = wait(g2b)
    g1b = onward(g2b, "g_from1b")
    arrived = wait(*arrived)
    total = wait(four(pieces[0], *arrived))
    beside = swap(total, "sum_x1", fx=1)
    g1a = wait(g1a)
    total = wait(add(total, wait(beside)))
    beside = swap(total, "sum_x2", fx=2)
    g1b = wait(g1b)
    total = wait(add(total, wait(beside)))
    beside = swap(total, "sum_z1", fz=1)
    g_own, g_send = wait(
        *lat_inverse(
            order.scalars, (g0a, g0b, g1a, g1b, g2a, g2b, g3a, g3b), g_over, lat_turned, owned
        )
    )
    g_recv = swap(g_send, "g_pair_back", fc=1)
    total = wait(add(total, wait(beside)))
    beside = swap(total, "sum_z2", fz=2)
    f_recv = wait(f_recv)
    block_out = wait(
        lon_inverse_fields(order.scalars, f_own, f_recv, inv_turned, field_in)
    )
    total = wait(add(total, wait(beside)))
    total = wait(jnp.stack([total, wait(swap(total, "all_core", fc=1))]))
    arrived = [swap(total, "all_y", fy=far) for far in (1, 2, 3)]
    g_recv = wait(g_recv)
    input_grad = wait(
        lon_inverse_grad(order.scalars, g_own, g_recv, fwd_turned, field_in, grad_out, gain)
    )
    arrived = wait(*arrived)
    weight_grads, bias_grads, gain_grad = place_sums(
        order.scalars, (total, *arrived), gain
    )
    return (block_out[None], input_grad[None], weight_grads, bias_grads, gain_grad)


def body(fields, cotangent, norm_gain, weights, biases, cutoffs):
    operands = (fields[0], cotangent[0], norm_gain, weights, biases, cutoffs)
    return whole_pass(OWNED, *operands)


OWNED = 16


def solution(mesh):
    placed = (P("dp", "row", None, None), P("dp", "row", None, None), P(), P(), P(), P())
    return jax.shard_map(
        body,
        mesh=mesh,
        in_specs=placed,
        out_specs=(P("dp", "row", None, None), P("dp", "row", None, None), P(), P(), P()),
        check_vma=False,
    )
```
